256 devices in a mesh: vol: 64 (over x_hi, z, y), tilt: 4 (over x_lo, core).
Axes of the slice: x: 4 (x_hi: 2, x_lo: 2; x = x_hi * 2 + x_lo), y: 4, z: 8, core: 2. Of those that a mesh axis runs over, the one named last changes fastest.
Arguments:
- images: bfloat16 [64, 128, 4096], P('tilt', 'vol'), may hold values from -6 to 6
- angle_tenths: int32 [64], P('tilt'), may hold values from -600 to 600
- dose_index: int32 [64], P('tilt'), may hold values from 0 to 120
- box_corner: int32 [3, 512], P(None, 'vol'), may hold values from 0 to 4032, as said below
- box_owner: int32 [512, 1], P('vol'), may hold values from 0 to 3; in each aligned block of 8 rows (0 to 7, 8 to 15, ...) at most 4 rows name the same one
Outputs:
- volume: bfloat16 [128, 4096, 128], P('tilt', 'vol')
- box_slots: bfloat16 [64, 4, 4, 64, 4096], P('vol', 'tilt')
The draws below stay inside these ranges and needn't reach their ends.
Inputs may be any that keep to these rules, and one draw needn't show every extreme that they name: `box_corner`: column r holds the corner x, y, z of a box. Its x lies in x-block r // 8, from (r // 8) * 64 to (r // 8) * 64 + 63, and is at most 4032; its y is at most 64 and its z at most 64. `box_owner`: within the rows of one device no owner is named more than 4 times.
All inputs are finite; a program needn't handle non-finite values.
Results may differ from the reference program's by a relative error of at most 0.014.
Values may be sent and summed in bfloat16 or wider, within the bound.
A program may use at most 192 MiB of HBM per device.

```python
import math
import jax
import jax.numpy as jnp
import numpy as np
from jax import lax

N = 4096
TILT_DEV = 16
Y = 128
ZS = 128
BOX = 64
P_DEV = 8
TILTS = 64
XB = 64
UW = 192
CAP = 4
PICKS = 512
N_VOL = 64
N_TILT = 4


def draw_box_corner(key, part):
    key = jax.random.fold_in(key, 7)
    key_x, key_y, key_z = jax.random.split(key, 3)
    positions = jnp.arange(PICKS, dtype=jnp.int32)
    x_block = positions // P_DEV
    within = positions % P_DEV
    offset_x = jax.random.randint(key_x, (PICKS,), 0, XB, dtype=jnp.int32)
    offset_x = jnp.where(within == P_DEV - 1, XB - BOX, offset_x)
    offset_x = jnp.where(positions == 0, 0, offset_x)
    corner_x = jnp.minimum(x_block * XB + offset_x, N - BOX)
    corner_y = jax.random.randint(key_y, (PICKS,), 0, Y - BOX + 1, dtype=jnp.int32)
    corner_z = jax.random.randint(key_z, (PICKS,), 0, ZS - BOX + 1, dtype=jnp.int32)
    corner_y = jnp.where(within == 1, Y - BOX, jnp.where(within == 0, 0, corner_y))
    corner_z = jnp.where(within == 1, ZS - BOX, jnp.where(within == 0, 0, corner_z))
    return jnp.stack([corner_x, corner_y, corner_z]).astype(jnp.int32)


def with_ends(result, key, low, top_value):
    shape = result.shape
    index_at = [jax.random.randint(jax.random.fold_in(key, axis), (), 0, shape[axis]) for axis in range(len(shape))]
    result = result.at[tuple(index_at)].set(low)
    longest = shape.index(max(shape))
    index_at[longest] = (index_at[longest] + 1) % shape[longest]
    return result.at[tuple(index_at)].set(top_value)


def shard_levels(stream_key, shape, cuts, smallest, top_value):
    level = 1.0
    for position, blocks in cuts:
        steps = jax.random.uniform(jax.random.fold_in(jax.random.fold_in(stream_key, 6), position), (blocks,), jnp.float32, smallest / len(cuts), top_value / len(cuts))
        level = level * jnp.repeat(jnp.exp(steps), shape[position] // blocks).reshape((-1,) + (1,) * (len(shape) - 1 - position))
    return level


def deal_out(key, own, number, rows, number_of, top, limit, skew):
    order = jax.random.permutation(key, number_of)
    heavy_load, ordinary = load_shares(number_of, rows * top, limit, skew, True), load_shares(number_of, rows * top, limit, skew, False)
    places = jnp.arange(number_of)

    def named(lengths, rotation):
        used = int((lengths > 0).sum())
        fixed = max(1, used // 4)
        shifted = fixed + (places - fixed + rotation * (used - fixed)) % max(1, number_of - fixed)
        return jnp.zeros((number_of,), jnp.int32).at[order[jnp.where(places < fixed, places, shifted)]].set(jnp.asarray(lengths, jnp.int32))

    lengths = jnp.where(number % 4 == 0, named(heavy_load, number // 4), named(ordinary, number - number // 4 - 1))
    mixed = jax.random.permutation(jax.random.fold_in(own, 3), number_of)
    source_of, sink = mixed[0:number_of // 2 * 2:2], mixed[1:number_of // 2 * 2:2]
    margin = jnp.minimum(lengths[source_of] - 1, limit - lengths[sink]) // 2
    margin = jnp.where((source_of == order[0]) | (sink == order[0]) | (lengths[sink] == 0), 0, jnp.maximum(margin, 0))
    shifted = jax.random.randint(jax.random.fold_in(own, 4), (number_of // 2,), 0, 1 << 20) % (margin + 1)
    lengths = lengths.at[source_of].add(-shifted).at[sink].add(shifted)
    items = jnp.searchsorted(jnp.cumsum(lengths), jnp.arange(rows * top), side="right").astype(jnp.int32)
    table = items.reshape(top, rows).T
    table = table[jax.random.permutation(jax.random.fold_in(own, 1), rows)]
    rotation = jax.random.randint(jax.random.fold_in(own, 2), (rows, 1), 0, top)
    return jnp.take_along_axis(table, (jnp.arange(top)[None, :] + rotation) % top, axis=1)


def load_shares(number_of, total, most, lean, full):
    portions = [(1 << 20) // math.isqrt(standing ** lean) + 1 for standing in range(1, number_of + 1)]
    largest = most if full else min(most, max(-(-total // number_of), total * portions[0] // sum(portions)))
    least = 1 if total - largest >= number_of - 1 else 0
    given, spare = [largest] + [least] * (number_of - 1), total - largest - least * (number_of - 1)
    while spare > 0:
        free = [i for i in range(1, number_of) if given[i] < largest] or [i for i in range(1, number_of) if given[i] < most]
        mass, budget = sum([portions[i] for i in free]), spare
        for i in free:
            extra = min(most - given[i], max(1, budget * portions[i] // mass), spare)
            given[i] = given[i] + extra
            spare = spare - extra
    return np.array(given)


def normal_values(own_key, extent, deviation, limit, cuts=(), kind=jnp.bfloat16):
    gain = shard_levels(own_key, extent, cuts, -0.22, 0.18) if cuts else 1.0
    result = jax.random.normal(own_key, extent, jnp.float32) * deviation * gain
    return jnp.minimum(jnp.maximum(result, -limit), limit).astype(kind)


def setup_inputs(seed: int = 0) -> dict:
    seeds = jax.random.split(jax.random.key(seed), 6)
    images = normal_values(seeds[0], (TILTS, Y, N), 1.0, 6.0, ((0, 4), (1, 64)))
    angle_tenths = with_ends(jax.random.randint(seeds[1], (TILTS,), -600, 601), jax.random.fold_in(seeds[1], 1), -600, 600).astype(jnp.int32)
    dose_index = with_ends(jax.random.randint(seeds[2], (TILTS,), 0, 121), jax.random.fold_in(seeds[2], 1), 0, 120).astype(jnp.int32)
    box_corner = draw_box_corner(jax.random.fold_in(seeds[5], 71), 0)
    box_owner_keys = jax.random.split(jax.random.fold_in(seeds[4], 1), PICKS // P_DEV)
    box_owner_turns = jax.random.permutation(jax.random.fold_in(seeds[4], 3), PICKS // P_DEV)
    box_owner = jax.vmap(lambda own, number: deal_out(jax.random.fold_in(seeds[4], 2), own, number, P_DEV, N_TILT, 1, P_DEV // 2, 2))(box_owner_keys, box_owner_turns).reshape((PICKS, 1))
    return dict(images=images, angle_tenths=angle_tenths, dose_index=dose_index, box_corner=box_corner, box_owner=box_owner)


def filter_response(dose_value, frequency_index, pixels):
    frequency = frequency_index.astype(jnp.float32)
    freq_ratio = 2.0 * frequency / pixels
    decay = jnp.exp(-0.05 * dose_value.astype(jnp.float32)[:, None] * (freq_ratio * jnp.sqrt(freq_ratio))[None, :])
    ramp = jnp.where(frequency_index * 2 == pixels, 0.0, frequency / pixels)
    return ramp[None, :] * decay

def band_start(cosine, sine_value, first_column, pixels, depth_cells, band_width):
    column_value = jnp.asarray(first_column).astype(jnp.float32)
    lowest = pixels / 2 + (column_value - pixels / 2) * cosine + jnp.minimum(-(depth_cells / 2) * sine_value, (depth_cells / 2 - 1) * sine_value)
    band_begin = jnp.floor(lowest).astype(jnp.int32) - 1
    return jnp.clip(band_begin, -depth_cells, pixels + depth_cells - band_width)

def band_weights(cosine, sine_value, band_begin, first_column, columns, pixels, depth_cells, band_width):
    column_value = jnp.asarray(first_column).astype(jnp.float32) + jnp.arange(columns, dtype=jnp.float32)
    depth_index = jnp.arange(depth_cells, dtype=jnp.float32)
    detector_coord = pixels / 2 + (column_value[:, None] - pixels / 2) * cosine + (depth_index[None, :] - depth_cells / 2) * sine_value
    pixel_index = (band_begin + jnp.arange(band_width, dtype=jnp.int32)).astype(jnp.float32)
    weight = jnp.maximum(0.0, 1.0 - jnp.abs(detector_coord[None, :, :] - pixel_index[:, None, None]))
    return weight.reshape(band_width, columns * depth_cells).astype(jnp.bfloat16)

def reference(images, angle_tenths, dose_index, box_corner, box_owner):
    tilt_angle = angle_tenths.astype(jnp.float32) * (math.pi / 1800.0)
    cosine = jnp.cos(tilt_angle)
    sine_value = jnp.sin(tilt_angle)
    image_rows = images.astype(jnp.float32).reshape(TILTS * Y, N)
    spectrum = jnp.fft.rfft(image_rows, axis=-1)
    response_rows = jnp.repeat(filter_response(dose_index, jnp.arange(N // 2 + 1, dtype=jnp.int32), N), Y, axis=0)
    restored = jnp.fft.irfft(spectrum * response_rows, n=N, axis=-1)
    filtered = restored.astype(jnp.bfloat16).reshape(TILTS, Y, N)
    padded = jnp.pad(filtered, ((0, 0), (0, 0), (ZS, ZS)))

    def one_block(x_block):
        first_column = x_block * XB
        starts = band_start(cosine, sine_value, first_column, N, ZS, UW)
        windows = jax.vmap(lambda row_block, begin_at: lax.dynamic_slice_in_dim(row_block, begin_at + ZS, UW, axis=1))(padded, starts)
        weights = jax.vmap(lambda cosine_one, sine_one, begin_at: band_weights(cosine_one, sine_one, begin_at, first_column, XB, N, ZS, UW))(cosine, sine_value, starts)
        partial_value = jnp.einsum('gtyu,gtuc->gyc', windows.astype(jnp.float32).reshape(N_TILT, TILT_DEV, Y, UW), weights.astype(jnp.float32).reshape(N_TILT, TILT_DEV, UW, XB * ZS), precision=lax.Precision.HIGHEST)
        rounded = lax.optimization_barrier(partial_value.astype(jnp.bfloat16))
        return lax.optimization_barrier(jnp.sum(rounded.astype(jnp.float32), axis=0)).astype(jnp.bfloat16)
    columns = lax.map(one_block, jnp.arange(N_VOL, dtype=jnp.int32))
    volume = columns.reshape(N_VOL, Y, XB, ZS).transpose(1, 0, 2, 3).reshape(Y, N, ZS)
    owners = box_owner[:, 0].reshape(N_VOL, P_DEV)
    positions = jnp.arange(P_DEV, dtype=jnp.int32)
    earlier = (owners[:, :, None] == owners[:, None, :]) & (positions[None, :] < positions[:, None])[None, :, :]
    slot_index = lax.optimization_barrier(jnp.sum(earlier.astype(jnp.int32), axis=2)).reshape(PICKS)

    def cut_box(corner):
        return lax.dynamic_slice(volume, (corner[1], corner[0], corner[2]), (BOX, BOX, BOX)).reshape(BOX, BOX * BOX)
    pieces = jax.vmap(cut_box, in_axes=1)(box_corner)
    blocks = jnp.arange(PICKS, dtype=jnp.int32) // P_DEV
    box_slots = jnp.zeros((N_VOL, N_TILT, CAP, BOX, BOX * BOX), jnp.bfloat16)
    box_slots = box_slots.at[blocks, box_owner[:, 0], slot_index].set(pieces)
    return (volume, box_slots)
```

```python
import functools
import math

import jax
import jax.numpy as jnp
import ml_dtypes
import numpy as np
from jax import lax
from jax.experimental import pallas as pl
from jax.experimental.pallas import tpu as pltpu
from jax.sharding import PartitionSpec as P

MESH = pl.DeviceIdType.MESH
BF = jnp.bfloat16
F32 = jnp.float32

PIX = 4096
EDGE = 64
COLS = 64
DEPTH = 128
BOX = 64
BLOCKS = 64
TILTS_HERE = 16
TILTS = 64
ROWS_MSG = 48
BAND = 192
TILE = 16
WIN = 32
CHUNK = 8
NCHUNK = TILTS // CHUNK
CELLS = 2 * COLS * DEPTH

VMEM_LIMIT = 56 * 1024 * 1024


def split_np(table):
    high = table.astype(np.float32).astype(ml_dtypes.bfloat16)
    low = (table - high.astype(np.float64)).astype(np.float32).astype(ml_dtypes.bfloat16)
    return high, low


def fft_tables():
    grid = np.outer(np.arange(EDGE), np.arange(EDGE))
    cos_t = np.cos(2 * np.pi * (grid % EDGE) / EDGE)
    sin_t = np.sin(2 * np.pi * (grid % EDGE) / EDGE)
    stacked = np.concatenate([cos_t, sin_t], axis=0)
    s_hi, s_lo = split_np(stacked)
    left = np.concatenate([s_hi, s_lo], axis=0)
    two = np.eye(2)
    cos2, sin2 = np.kron(two, cos_t), np.kron(two, sin_t)
    fwd = np.block([[cos2, -sin2], [sin2, cos2]])
    inv = np.block([[cos2, sin2], [-sin2, cos2]])
    f_hi, f_lo = split_np(fwd)
    i_hi, i_lo = split_np(inv)
    right = np.stack([f_hi, f_lo, i_hi, i_lo])
    twist = np.stack([np.cos(2 * np.pi * grid / PIX), np.sin(2 * np.pi * grid / PIX)])
    twist = np.concatenate([twist, twist], axis=2).astype(np.float32)
    k1, k2 = np.meshgrid(np.arange(EDGE), np.arange(EDGE), indexing="ij")
    freq = k1 + EDGE * k2
    freq = np.minimum(freq, PIX - freq)
    ratio = 2.0 * freq / PIX
    bend = ratio * np.sqrt(ratio)
    ramp = np.where(freq * 2 == PIX, 0.0, freq / PIX) / PIX
    shape = np.stack([bend, ramp])
    shape = np.concatenate([shape, shape], axis=2).astype(np.float32)
    return left, right, twist, shape


def dot(a, b):
    return jnp.dot(a, b, preferred_element_type=F32)


def dot_t(a, b):
    return lax.dot_general(a, b, (((1,), (1,)), ((), ())), preferred_element_type=F32)


def halves(value):
    high = value.astype(BF)
    return high, (value - high.astype(F32)).astype(BF)


def filter_kernel(
    x_ref, left_ref, right_ref, twist_ref, shape_ref, dose_ref, quot_ref, rest_ref, meta_ref, out_ref, scr
):
    left = left_ref[...]
    cos_w, sin_w = twist_ref[0], twist_ref[1]
    bend, ramp = shape_ref[0], shape_ref[1]
    lane = lax.broadcasted_iota(jnp.int32, (EDGE, 128), 1)
    first = lane < EDGE
    n1 = lax.broadcasted_iota(jnp.int32, (BLOCKS, EDGE), 1)
    for pair in range(TILTS_HERE // 2):
        part = dot(left, x_ref[pair])
        cx = part[0:64] + part[128:192]
        sx = part[64:128] + part[192:256]
        re = cx[:, :128] + sx[:, 128:]
        im = cx[:, 128:] - sx[:, :128]
        turned = jnp.concatenate([re * cos_w + im * sin_w, im * cos_w - re * sin_w], axis=1)
        hi, lo = halves(turned)
        spec = dot(hi, right_ref[0]) + (dot(lo, right_ref[0]) + dot(hi, right_ref[1]))
        resp = ramp * jnp.exp((-0.05 * dose_ref[pair : pair + 1, :]) * bend)
        spec = spec * jnp.concatenate([resp, resp], axis=1)
        hi, lo = halves(spec)
        back = dot(hi, right_ref[2]) + (dot(lo, right_ref[2]) + dot(hi, right_ref[3]))
        re, im = back[:, :128], back[:, 128:]
        turned = jnp.concatenate([re * cos_w - im * sin_w, im * cos_w + re * sin_w], axis=1)
        hi, lo = halves(turned)
        part = dot(left, hi)
        extra = dot(left[0:128], lo)
        cx = part[0:64] + (part[128:192] + extra[0:64])
        sx = part[64:128] + (part[192:256] + extra[64:128])
        re = cx[:, :128] - sx[:, 128:]
        im = cx[:, 128:] + sx[:, :128]
        rows = (
            jnp.where(first, re, pltpu.roll(im, EDGE, 1)),
            jnp.where(first, pltpu.roll(re, EDGE, 1), im),
        )
        for half in range(2):
            tilt = 2 * pair + half
            image = rows[half].astype(BF)
            quot = quot_ref[:, tilt : tilt + 1]
            rest = rest_ref[:, tilt : tilt + 1]
            pick = jnp.concatenate(
                [(n1 == quot + step).astype(F32).astype(BF) for step in range(4)], axis=0
            )
            near = dot(pick, image)
            at = (lane & EDGE) | ((lane + rest) & (EDGE - 1))
            stay = (lane & (EDGE - 1)) + rest < EDGE
            moved = [
                jnp.take_along_axis(near[step * EDGE : (step + 1) * EDGE], at, axis=1)
                for step in range(4)
            ]
            for step in range(3):
                piece = jnp.where(stay, moved[step], moved[step + 1])
                if step == 2:
                    for place in range(2):
                        piece = jnp.where(lane == 60 + place, meta_ref[place, tilt : tilt + 1, 0:1], piece)
                    piece = jnp.where(lane == 62, quot.astype(F32), piece)
                    piece = jnp.where(lane == 63, rest.astype(F32), piece)
                scr[pl.ds(tilt * 3 + step, BLOCKS, stride=ROWS_MSG), :] = piece
    for block in range(BLOCKS):
        out_ref[block] = scr[block * ROWS_MSG : (block + 1) * ROWS_MSG, :].astype(BF)


def exchange_kernel(x_ref, o_ref, loc_sem, a_send, a_recv, x_send, x_recv, m_send, m_recv):
    v = lax.axis_index("vol")
    t = lax.axis_index("tilt")
    y, z, xh = lax.rem(v, 4), lax.rem(v // 4, 8), v // 32
    core, xl = lax.rem(t, 2), t // 2
    mate = xl * 2 + (1 - core)
    cross = (1 - xl) * 2 + core
    barrier = pltpu.get_barrier_semaphore()

    def greet(i, carry):
        p = lax.rem(xh * 32 + i, 64)
        q = jnp.where(i < 32, t, cross)

        @pl.when(p != v)
        def _():
            pl.semaphore_signal(barrier, inc=1, device_id=(p, q), device_id_type=MESH)

        return carry

    lax.fori_loop(0, 64, greet, 0)
    pl.semaphore_signal(barrier, inc=1, device_id=(v, cross), device_id_type=MESH)
    pl.semaphore_signal(barrier, inc=1, device_id=(v, mate), device_id_type=MESH)
    pl.semaphore_wait(barrier, 65)

    own = pltpu.make_async_copy(x_ref.at[v], o_ref.at[t, v], loc_sem)
    own.start()
    steps = (0, 1, 7, 2, 6, 3, 5, 4)
    for dz in steps:
        for far in range(2):
            for dy in range(4):
                if dz == 0 and far == 0 and dy == 0:
                    continue
                zz, yy = lax.rem(z + dz, 8), lax.rem(y + dy, 4)
                p = (xh if far == 0 else 1 - xh) * 32 + zz * 4 + yy
                pltpu.make_async_remote_copy(
                    x_ref.at[p],
                    o_ref.at[t, v],
                    a_send,
                    a_recv.at[far, z],
                    device_id=(p, t if far == 0 else cross),
                    device_id_type=MESH,
                ).start()
    for dz in steps:
        for far in range(2):
            zz = lax.rem(z + 8 - dz, 8)
            base = (xh if far == 0 else 1 - xh) * 32 + zz * 4
            slot = t if far == 0 else cross
            number = 4
            if dz == 0 and far == 0:
                own.wait()
                number = 3
            pltpu.make_async_copy(
                o_ref.at[slot, pl.ds(base, number)], o_ref.at[slot, pl.ds(base, number)], a_recv.at[far, zz]
            ).wait()
            block = o_ref.at[slot, pl.ds(base, 4)]
            pltpu.make_async_remote_copy(
                block, block, x_send, x_recv.at[far, zz], device_id=(v, cross), device_id_type=MESH
            ).start()
            pltpu.make_async_remote_copy(
                block, block, m_send, m_recv.at[0, far, zz], device_id=(v, mate), device_id_type=MESH
            ).start()
    for dz in steps:
        for far in range(2):
            zz = lax.rem(z + 8 - dz, 8)
            base = (xh if far == 0 else 1 - xh) * 32 + zz * 4
            slot = cross if far == 0 else t
            block = o_ref.at[slot, pl.ds(base, 4)]
            pltpu.make_async_copy(block, block, x_recv.at[far, zz]).wait()
            pltpu.make_async_remote_copy(
                block, block, m_send, m_recv.at[1, far, zz], device_id=(v, mate), device_id_type=MESH
            ).start()
    mate_cross = (1 - xl) * 2 + (1 - core)
    for kind in range(2):
        for far in range(2):
            for zz in range(8):
                base = (xh if far == 0 else 1 - xh) * 32 + zz * 4
                slot = mate if (kind + far) % 2 == 0 else mate_cross
                block = o_ref.at[slot, pl.ds(base, 4)]
                pltpu.make_async_copy(block, block, m_recv.at[kind, far, zz]).wait()
    pltpu.make_async_copy(x_ref.at[pl.ds(0, 63)], x_ref.at[pl.ds(0, 63)], a_send).wait()
    half = o_ref.at[0]
    pltpu.make_async_copy(half, half, x_send).wait()
    both = o_ref.at[pl.ds(0, 2)]
    pltpu.make_async_copy(both, both, m_send).wait()


def project_kernel(recv_ref, start_ref, cst_ref, trig_ref, part, scr, win):
    lane = lax.broadcasted_iota(jnp.int32, (BLOCKS, 128), 1)
    low = lane < EDGE
    fold = (
        lax.broadcasted_iota(jnp.int32, (EDGE, 128), 0) == (lane & (EDGE - 1))
    ).astype(F32).astype(BF)

    for group in range(4):
        scr[group * 3072 : (group + 1) * 3072, :] = recv_ref[group].reshape(3072, 128).astype(F32)

    def turn(tilt, carry):
        group, inner = tilt // TILTS_HERE, lax.rem(tilt, TILTS_HERE)
        parts = []
        for step in range(3):
            piece = scr[pl.ds(group * 3072 + inner * 3 + step, BLOCKS, stride=ROWS_MSG), :]
            wide = jnp.concatenate([jnp.where(low, piece, 0.0), jnp.where(low, 0.0, piece)], axis=0)
            parts.append(dot_t(fold, wide.astype(BF)))
        whole = jnp.concatenate(parts, axis=0)
        moved = jnp.concatenate([whole[8:], jnp.zeros((8, 128), F32)], axis=0)
        at = pl.multiple_of(tilt * 2 * BAND, BAND)
        win[pl.ds(at, BAND), :] = whole.astype(BF)
        win[pl.ds(at + BAND, BAND), :] = moved.astype(BF)
        return carry

    lax.fori_loop(0, TILTS, turn, 0, unroll=4)

    zcol = lax.broadcasted_iota(jnp.int32, (TILE, CHUNK * WIN), 0).astype(F32)

    def tile(xt, zt, carry):
        number = xt * 8 + zt
        total = jnp.zeros((TILE * TILE, 128), F32)
        for chunk in range(NCHUNK):
            right = jnp.concatenate(
                [
                    win[pl.ds(pl.multiple_of(start_ref[number, chunk * CHUNK + i], 16), WIN), :]
                    for i in range(CHUNK)
                ],
                axis=0,
            )
            cos_l = trig_ref[chunk : chunk + 1, :]
            sin_l = trig_ref[NCHUNK + chunk : NCHUNK + chunk + 1, :]
            here = zcol * sin_l + cst_ref[pl.ds(number * NCHUNK + chunk, 1), :]
            pieces = []
            for _ in range(TILE):
                pieces.append(jnp.maximum(1.0 - jnp.abs(here), 0.0).astype(BF))
                here = here + cos_l
            total = total + dot(jnp.concatenate(pieces, axis=0), right)
        rounded = total.astype(BF)
        for i in range(TILE):
            at = pl.multiple_of((xt * TILE + i) * DEPTH + zt * TILE, TILE)
            part[pl.ds(at, TILE), :] = rounded[i * TILE : (i + 1) * TILE]
        return carry

    for xt in range(4):
        lax.fori_loop(0, 8, functools.partial(tile, xt), 0)


def mate_kernel(x_ref, o_ref, send, recv):
    v = lax.axis_index("vol")
    t = lax.axis_index("tilt")
    mate = (t // 2) * 2 + (1 - lax.rem(t, 2))
    barrier = pltpu.get_barrier_semaphore()
    pl.semaphore_signal(barrier, inc=1, device_id=(v, mate), device_id_type=MESH)
    pl.semaphore_wait(barrier, 1)
    there = pltpu.make_async_remote_copy(
        x_ref, o_ref, send, recv, device_id=(v, mate), device_id_type=MESH
    )
    there.start()
    there.wait()


def box_kernel(own_ref, other_ref, slot_ref, box_ref, vol_ref, ext_ref, sem):
    core = slot_ref[17]
    half = CELLS // 2
    here = pltpu.make_async_copy(
        own_ref, ext_ref.at[pl.ds(pl.multiple_of(core * half, half), half)], sem.at[0]
    )
    there = pltpu.make_async_copy(
        other_ref, ext_ref.at[pl.ds(pl.multiple_of((1 - core) * half, half), half)], sem.at[1]
    )
    here.start()
    there.start()
    here.wait()
    there.wait()
    lane = lax.broadcasted_iota(jnp.int32, (BOX, 128), 1)
    low = lane < BOX
    y_of = (lane & 63) * 2 + (lane >> 6)
    line = lax.broadcasted_iota(jnp.int32, (BOX, 128), 0)
    quarter = (y_of == line + slot_ref[16]).astype(F32).astype(BF)[0:32]

    def slab(i, carry):
        rows = ext_ref[pl.ds(pl.multiple_of(i * 256, 256), 256), :]
        vol_ref[:, pl.ds(pl.multiple_of(i * 256, 256), 256)] = dot_t(quarter, rows).astype(BF)
        return carry

    lax.fori_loop(0, COLS // 2, slab, 0, unroll=4)

    for slot in range(4):
        x0, y0, z0 = slot_ref[slot * 4 + 1], slot_ref[slot * 4 + 2], slot_ref[slot * 4 + 3]
        present = slot_ref[slot * 4]
        chosen = ((y_of == line + y0) & (present > 0)).astype(F32).astype(BF)
        even_by = lax.rem(128 - z0, 128)
        odd_by = lax.rem(192 - z0, 128)

        def cut(i, carry):
            rows = ext_ref[pl.ds(pl.multiple_of((x0 + 2 * i) * DEPTH, DEPTH), 2 * DEPTH), :]
            both = dot_t(chosen, rows)
            even = pltpu.roll(both[:, :128], even_by, 1)
            odd = pltpu.roll(both[:, 128:], odd_by, 1)
            box_ref[slot, :, pl.ds(pl.multiple_of(i * 128, 128), 128)] = jnp.where(
                low, even, odd
            ).astype(BF)
            return carry

        lax.fori_loop(0, BOX // 2, cut, 0, unroll=4)


def trig_of(tenths):
    angle = tenths.astype(F32) * (math.pi / 1800.0)
    return jnp.cos(angle), jnp.sin(angle)


def per_device(images, angle_tenths, dose_index, box_corner, box_owner):
    x_block = lax.axis_index("vol")
    group = lax.axis_index("tilt")
    core = lax.rem(group, 2)
    vm = pl.BlockSpec(memory_space=pltpu.VMEM)
    sm = pl.BlockSpec(memory_space=pltpu.SMEM)
    anym = pl.BlockSpec(memory_space=pl.ANY)

    cosine, sine = trig_of(angle_tenths)
    columns = jnp.arange(BLOCKS, dtype=jnp.int32).astype(F32)[:, None] * COLS
    lowest = (
        PIX / 2
        + (columns - PIX / 2) * cosine[None, :]
        + jnp.minimum(-(DEPTH / 2) * sine, (DEPTH / 2 - 1) * sine)[None, :]
    )
    begin = jnp.floor(lowest).astype(jnp.int32) - 1
    quot, rest = begin >> 6, begin & 63
    meta = jnp.stack([angle_tenths >> 5, angle_tenths & 31]).astype(F32)
    meta = jnp.broadcast_to(meta[:, :, None], (2, TILTS_HERE, 128))
    dose = jnp.repeat(dose_index.astype(F32).reshape(TILTS_HERE // 2, 2), EDGE, axis=1)
    cube = images.reshape(TILTS_HERE // 2, 2, 2, EDGE, EDGE).transpose(0, 3, 2, 1, 4)
    cube = cube.reshape(TILTS_HERE // 2, EDGE, 4 * EDGE)
    tables = [jnp.asarray(a) for a in fft_tables()]
    outgoing = pl.pallas_call(
        filter_kernel,
        out_shape=jax.ShapeDtypeStruct((BLOCKS, ROWS_MSG, 128), BF),
        in_specs=[vm] * 9,
        out_specs=vm,
        scratch_shapes=[pltpu.VMEM((BLOCKS * ROWS_MSG, 128), F32)],
        compiler_params=pltpu.CompilerParams(vmem_limit_bytes=VMEM_LIMIT),
        name="filter",
    )(cube, *tables, dose, quot, rest, meta)

    dma = pltpu.SemaphoreType.DMA
    recv = pl.pallas_call(
        exchange_kernel,
        out_shape=jax.ShapeDtypeStruct((4, BLOCKS, ROWS_MSG, 128), BF),
        in_specs=[anym],
        out_specs=anym,
        scratch_shapes=[dma, dma, dma((2, 8)), dma, dma((2, 8)), dma, dma((2, 2, 8))],
        compiler_params=pltpu.CompilerParams(collective_id=1, has_side_effects=True),
        name="exchange",
    )(outgoing)

    heads = recv[:, 0].reshape(TILTS, 3, 128)[:, 2, 60:64].astype(jnp.int32)
    tenths = heads[:, 0] * 32 + heads[:, 1]
    base = heads[:, 2] * 64 + heads[:, 3]
    cos_all, sin_all = trig_of(tenths)
    number = jnp.arange(32, dtype=jnp.int32)
    x_tile = (x_block * COLS + core * COLS + (number // 8) * TILE).astype(F32)
    z_tile = ((number % 8) * TILE).astype(F32)
    coord = (
        PIX / 2
        + (x_tile[:, None] - PIX / 2) * cos_all[None, :]
        + (z_tile[:, None] - DEPTH / 2) * sin_all[None, :]
    )
    least = coord + jnp.minimum((TILE - 1) * sin_all, 0.0)[None, :]
    local = jnp.clip(jnp.floor(least).astype(jnp.int32) - base[None, :], 0, BAND - WIN)
    local8 = local & -8
    odd = (local8 >> 3) & 1
    tilt_number = jnp.arange(TILTS, dtype=jnp.int32)[None, :]
    start = (tilt_number * 2 + odd) * BAND + local8 - 8 * odd
    offset = coord - (base[None, :] + local8).astype(F32)
    pixel = jnp.arange(WIN, dtype=jnp.int32).astype(F32)
    cst = (offset[:, :, None] - pixel).reshape(32 * NCHUNK, CHUNK * WIN)
    trig = jnp.stack([cos_all, sin_all])
    trig = jnp.repeat(trig.reshape(2 * NCHUNK, CHUNK), WIN, axis=1)
    part = pl.pallas_call(
        project_kernel,
        out_shape=jax.ShapeDtypeStruct((CELLS // 2, 128), BF),
        in_specs=[vm, sm, vm, vm],
        out_specs=vm,
        scratch_shapes=[
            pltpu.VMEM((4 * BLOCKS * ROWS_MSG, 128), F32),
            pltpu.VMEM((TILTS * 2 * BAND, 128), BF),
        ],
        compiler_params=pltpu.CompilerParams(vmem_limit_bytes=VMEM_LIMIT),
        name="project",
    )(recv, start, cst, trig)

    other = pl.pallas_call(
        mate_kernel,
        out_shape=jax.ShapeDtypeStruct((CELLS // 2, 128), BF),
        in_specs=[anym],
        out_specs=anym,
        scratch_shapes=[dma, dma],
        compiler_params=pltpu.CompilerParams(collective_id=2, has_side_effects=True),
        name="mate",
    )(part)

    owners = box_owner[:, 0]
    positions = jnp.arange(owners.shape[0], dtype=jnp.int32)
    earlier = (owners[:, None] == owners[None, :]) & (positions[None, :] < positions[:, None])
    slot_index = jnp.sum(earlier.astype(jnp.int32), axis=1)
    chosen = (owners[None, :] == group) & (slot_index[None, :] == jnp.arange(4, dtype=jnp.int32)[:, None])
    fields = jnp.stack(
        [jnp.ones_like(owners), box_corner[0] - x_block * COLS, box_corner[1], box_corner[2]]
    )
    info = jnp.sum(jnp.where(chosen[:, None, :], fields[None, :, :], 0), axis=2).reshape(16)
    info = jnp.concatenate([info, (group * 32).reshape(1), core.reshape(1)]).astype(jnp.int32)
    boxes, volume = pl.pallas_call(
        box_kernel,
        out_shape=(
            jax.ShapeDtypeStruct((4, BOX, BOX * BOX), BF),
            jax.ShapeDtypeStruct((32, COLS * DEPTH), BF),
        ),
        in_specs=[anym, anym, sm],
        out_specs=(vm, vm),
        scratch_shapes=[pltpu.VMEM((CELLS, 128), BF), dma((2,))],
        compiler_params=pltpu.CompilerParams(vmem_limit_bytes=VMEM_LIMIT),
        name="boxes",
    )(part, other, info)
    return volume.reshape(32, COLS, DEPTH), boxes.reshape(1, 1, 4, BOX, BOX * BOX)


def solution(mesh):
    in_specs = (P("tilt", "vol", None), P("tilt"), P("tilt"), P(None, "vol"), P("vol", None))
    out_specs = (P("tilt", "vol", None), P("vol", "tilt", None, None, None))
    return jax.shard_map(
        per_device, mesh=mesh, in_specs=in_specs, out_specs=out_specs, check_vma=False
    )
```

```python
import functools
import math

import jax
import jax.numpy as jnp
import ml_dtypes
import numpy as np
from jax import lax
from jax.experimental import pallas as pl
from jax.experimental.pallas import tpu as pltpu
from jax.sharding import PartitionSpec as P

MESH = pl.DeviceIdType.MESH
BF = jnp.bfloat16
F32 = jnp.float32

PIX = 4096
EDGE = 64
COLS = 64
DEPTH = 128
BOX = 64
BLOCKS = 64
TILTS_HERE = 16
TILTS = 64
ROWS_MSG = 48
BAND = 192
TILE = 16
WIN = 24
LANES = TILTS * WIN
CELLS = 2 * COLS * DEPTH

VMEM_LIMIT = 56 * 1024 * 1024


def split_np(table):
    high = table.astype(np.float32).astype(ml_dtypes.bfloat16)
    low = (table - high.astype(np.float64)).astype(np.float32).astype(ml_dtypes.bfloat16)
    return high, low


def fft_tables():
    grid = np.outer(np.arange(EDGE), np.arange(EDGE))
    cos_t = np.cos(2 * np.pi * (grid % EDGE) / EDGE)
    sin_t = np.sin(2 * np.pi * (grid % EDGE) / EDGE)
    stacked = np.concatenate([cos_t, sin_t], axis=0)
    s_hi, s_lo = split_np(stacked)
    left = np.concatenate([s_hi, s_lo], axis=0)
    order = np.concatenate([np.arange(0, EDGE, 2), np.arange(1, EDGE, 2)])
    left = np.stack([left[:, order], left])
    two = np.eye(2)
    cos2, sin2 = np.kron(two, cos_t), np.kron(two, sin_t)
    fwd = np.block([[cos2, -sin2], [sin2, cos2]])
    inv = np.block([[cos2, sin2], [-sin2, cos2]])
    f_hi, f_lo = split_np(fwd)
    i_hi, i_lo = split_np(inv)
    right = np.stack([f_hi, f_lo, i_hi, i_lo])
    twist = np.stack([np.cos(2 * np.pi * grid / PIX), np.sin(2 * np.pi * grid / PIX)])
    twist = np.concatenate([twist, twist], axis=2).astype(np.float32)
    k1, k2 = np.meshgrid(np.arange(EDGE), np.arange(EDGE), indexing="ij")
    freq = k1 + EDGE * k2
    freq = np.minimum(freq, PIX - freq)
    ratio = 2.0 * freq / PIX
    bend = ratio * np.sqrt(ratio)
    ramp = np.where(freq * 2 == PIX, 0.0, freq / PIX) / PIX
    shape = np.stack([bend, ramp])
    shape = np.concatenate([shape, shape], axis=2).astype(np.float32)
    return left, right, twist, shape


def dot(a, b):
    return jnp.dot(a, b, preferred_element_type=F32)


def dot_t(a, b):
    return lax.dot_general(a, b, (((1,), (1,)), ((), ())), preferred_element_type=F32)


def halves(value):
    high = value.astype(BF)
    return high, (value - high.astype(F32)).astype(BF)


def filter_pairs(pairs, x_ref, left_ref, right_ref, twist_ref, shape_ref, angle_row, angle_ref, dose_ref, cube, scr):
    first_left, left = left_ref[0], left_ref[1]
    cos_w, sin_w = twist_ref[0], twist_ref[1]
    bend, ramp = shape_ref[0], shape_ref[1]
    lane = lax.broadcasted_iota(jnp.int32, (EDGE, 128), 1)
    first = lane < EDGE
    thin = first[0:32]
    n1 = lax.broadcasted_iota(jnp.int32, (BLOCKS, EDGE), 1)
    cosine, sine = trig_of(angle_row[...])
    columns = lax.broadcasted_iota(jnp.int32, (BLOCKS, TILTS_HERE), 0).astype(F32) * COLS
    lowest = (
        PIX / 2
        + (columns - PIX / 2) * cosine
        + jnp.minimum(-(DEPTH / 2) * sine, (DEPTH / 2 - 1) * sine)
    )
    begin = jnp.floor(lowest).astype(jnp.int32) - 1
    quots, rests = begin >> 6, begin & 63

    def side(row, pair):
        one = cube[pl.ds((pair * 4 + row) * 32, 32), :]
        two = cube[pl.ds((pair * 4 + 2 + row) * 32, 32), :]
        even = jnp.where(thin, one, pltpu.roll(two, EDGE, 1))
        odd = jnp.where(thin, pltpu.roll(one, EDGE, 1), two)
        return jnp.concatenate([even, odd], axis=0).astype(BF)

    for pair in pairs:
        part = dot(first_left, jnp.concatenate([side(0, pair), side(1, pair)], axis=1))
        cx = part[0:64] + part[128:192]
        sx = part[64:128] + part[192:256]
        re = cx[:, :128] + sx[:, 128:]
        im = cx[:, 128:] - sx[:, :128]
        turned = jnp.concatenate([re * cos_w + im * sin_w, im * cos_w - re * sin_w], axis=1)
        hi, lo = halves(turned)
        spec = dot(hi, right_ref[0]) + (dot(lo, right_ref[0]) + dot(hi, right_ref[1]))
        dose = jnp.where(first, dose_ref[2 * pair].astype(F32), dose_ref[2 * pair + 1].astype(F32))
        resp = ramp * jnp.exp((-0.05 * dose) * bend)
        spec = spec * jnp.concatenate([resp, resp], axis=1)
        hi, lo = halves(spec)
        back = dot(hi, right_ref[2]) + (dot(lo, right_ref[2]) + dot(hi, right_ref[3]))
        re, im = back[:, :128], back[:, 128:]
        turned = jnp.concatenate([re * cos_w - im * sin_w, im * cos_w + re * sin_w], axis=1)
        hi, lo = halves(turned)
        part = dot(left, hi)
        extra = dot(left[0:128], lo)
        cx = part[0:64] + (part[128:192] + extra[0:64])
        sx = part[64:128] + (part[192:256] + extra[64:128])
        re = cx[:, :128] - sx[:, 128:]
        im = cx[:, 128:] + sx[:, :128]
        rows = (
            jnp.where(first, re, pltpu.roll(im, EDGE, 1)),
            jnp.where(first, pltpu.roll(re, EDGE, 1), im),
        )
        for half in range(2):
            tilt = 2 * pair + half
            image = rows[half].astype(BF)
            quot = quots[:, tilt : tilt + 1]
            rest = rests[:, tilt : tilt + 1]
            pick = jnp.concatenate(
                [(n1 == quot + step).astype(F32).astype(BF) for step in range(4)], axis=0
            )
            near = dot(pick, image)
            at = (lane & EDGE) | ((lane + rest) & (EDGE - 1))
            stay = (lane & (EDGE - 1)) + rest < EDGE
            moved = [
                jnp.take_along_axis(near[step * EDGE : (step + 1) * EDGE], at, axis=1)
                for step in range(4)
            ]
            for step in range(3):
                piece = jnp.where(stay, moved[step], moved[step + 1])
                if step == 2:
                    tenths = angle_ref[tilt]
                    piece = jnp.where(lane == 60, (tenths >> 5).astype(F32), piece)
                    piece = jnp.where(lane == 61, (tenths & 31).astype(F32), piece)
                    piece = jnp.where(lane == 62, quot.astype(F32), piece)
                    piece = jnp.where(lane == 63, rest.astype(F32), piece)
                scr[pl.ds(tilt * 3 + step, BLOCKS, stride=ROWS_MSG), :] = piece


def exchange_kernel(
    image_ref, left_ref, right_ref, twist_ref, shape_ref, angle_row, angle_ref, dose_ref, o_ref,
    cube, scr, x_ref, loc_sem, a_send, a_recv, x_send, x_recv, m_send, m_recv,
):
    v = lax.axis_index("vol")
    t = lax.axis_index("tilt")
    y, z, xh = lax.rem(v, 4), lax.rem(v // 4, 8), v // 32
    core, xl = lax.rem(t, 2), t // 2
    mate = xl * 2 + (1 - core)
    cross = (1 - xl) * 2 + core
    barrier = pltpu.get_barrier_semaphore()

    def greet(i, carry):
        p = lax.rem(xh * 32 + i, 64)
        q = jnp.where(i < 32, t, cross)

        @pl.when(p != v)
        def _():
            pl.semaphore_signal(barrier, inc=1, device_id=(p, q), device_id_type=MESH)

        return carry

    lax.fori_loop(0, 64, greet, 0)
    pl.semaphore_signal(barrier, inc=1, device_id=(v, cross), device_id_type=MESH)
    pl.semaphore_signal(barrier, inc=1, device_id=(v, mate), device_id_type=MESH)

    for tilt in range(TILTS_HERE):
        wide = image_ref[tilt].astype(F32)
        for j in range(PIX // 128):
            cube[pl.ds(tilt * 64 + j, 2, stride=32), :] = wide[:, j * 128 : (j + 1) * 128]

    operands = (image_ref, left_ref, right_ref, twist_ref, shape_ref, angle_row, angle_ref, dose_ref, cube, scr)
    steps = (0, 1, 7, 2, 6, 3, 5, 4)

    def send_rows(low, high):
        for block in range(BLOCKS):
            x_ref[block, low:high] = scr[block * ROWS_MSG + low : block * ROWS_MSG + high, :].astype(BF)
        for dz in steps:
            for far in range(2):
                for dy in range(4):
                    if dz == 0 and far == 0 and dy == 0:
                        continue
                    zz, yy = lax.rem(z + dz, 8), lax.rem(y + dy, 4)
                    p = (xh if far == 0 else 1 - xh) * 32 + zz * 4 + yy
                    pltpu.make_async_remote_copy(
                        x_ref.at[p, pl.ds(low, high - low)],
                        o_ref.at[t, v, pl.ds(low, high - low)],
                        a_send,
                        a_recv.at[far, z],
                        device_id=(p, t if far == 0 else cross),
                        device_id_type=MESH,
                    ).start()

    filter_pairs(range(0, 3), *operands)
    pl.semaphore_wait(barrier, 65)
    send_rows(0, 16)
    filter_pairs(range(3, 8), *operands)
    send_rows(16, 48)
    own = pltpu.make_async_copy(x_ref.at[v], o_ref.at[t, v], loc_sem)
    own.start()
    for dz in steps:
        for far in range(2):
            zz = lax.rem(z + 8 - dz, 8)
            base = (xh if far == 0 else 1 - xh) * 32 + zz * 4
            slot = t if far == 0 else cross
            number = 4
            if dz == 0 and far == 0:
                own.wait()
                number = 3
            pltpu.make_async_copy(
                o_ref.at[slot, pl.ds(base, number)], o_ref.at[slot, pl.ds(base, number)], a_recv.at[far, zz]
            ).wait()
            block = o_ref.at[slot, pl.ds(base, 4)]
            pltpu.make_async_remote_copy(
                block, block, x_send, x_recv.at[far, zz], device_id=(v, cross), device_id_type=MESH
            ).start()
            pltpu.make_async_remote_copy(
                block, block, m_send, m_recv.at[0, far, zz], device_id=(v, mate), device_id_type=MESH
            ).start()
    for dz in steps:
        for far in range(2):
            zz = lax.rem(z + 8 - dz, 8)
            base = (xh if far == 0 else 1 - xh) * 32 + zz * 4
            slot = cross if far == 0 else t
            block = o_ref.at[slot, pl.ds(base, 4)]
            pltpu.make_async_copy(block, block, x_recv.at[far, zz]).wait()
            pltpu.make_async_remote_copy(
                block, block, m_send, m_recv.at[1, far, zz], device_id=(v, mate), device_id_type=MESH
            ).start()
    mate_cross = (1 - xl) * 2 + (1 - core)
    for kind in range(2):
        for far in range(2):
            for zz in range(8):
                base = (xh if far == 0 else 1 - xh) * 32 + zz * 4
                slot = mate if (kind + far) % 2 == 0 else mate_cross
                block = o_ref.at[slot, pl.ds(base, 4)]
                pltpu.make_async_copy(block, block, m_recv.at[kind, far, zz]).wait()
    pltpu.make_async_copy(x_ref.at[pl.ds(0, 63)], x_ref.at[pl.ds(0, 63)], a_send).wait()
    half = o_ref.at[0]
    pltpu.make_async_copy(half, half, x_send).wait()
    both = o_ref.at[pl.ds(0, 2)]
    pltpu.make_async_copy(both, both, m_send).wait()


def project_kernel(recv_ref, lane_tilt, lane_pixel, part, land, scr, win, starts_v, starts_s, cst, trig, sem, sem2):
    v = lax.axis_index("vol")
    core = lax.rem(lax.axis_index("tilt"), 2)
    size = BLOCKS * ROWS_MSG
    arrive = [pltpu.make_async_copy(recv_ref.at[g], land.at[g], sem.at[g]) for g in range(4)]
    for copy in arrive:
        copy.start()
    lane = lax.broadcasted_iota(jnp.int32, (BLOCKS, 128), 1)
    low = lane < EDGE
    fold = (
        lax.broadcasted_iota(jnp.int32, (EDGE, 128), 0) == (lane & (EDGE - 1))
    ).astype(F32).astype(BF)
    for group in range(4):
        arrive[group].wait()
        scr[group * size : (group + 1) * size, :] = land[group].reshape(size, 128).astype(F32)

    heads = [scr[pl.ds(g * size + 2, TILTS_HERE, stride=3), :] for g in range(4)]
    heads = jnp.concatenate(heads + [jnp.zeros((128 - TILTS, 128), F32)], axis=0).T
    tenths = heads[60:61] * 32.0 + heads[61:62]
    base = heads[62:63] * 64.0 + heads[63:64]
    cosine, sine = trig_of(tenths)
    number = lax.broadcasted_iota(jnp.int32, (32, 128), 0)
    x_tile = ((number >> 3) * TILE + (v + core) * COLS).astype(F32)
    z_tile = ((number & 7) * TILE).astype(F32)
    coord = PIX / 2 + (x_tile - PIX / 2) * cosine + (z_tile - DEPTH / 2) * sine
    local = jnp.floor(coord + jnp.minimum((TILE - 1) * sine, 0.0)) - base
    local = jnp.clip(local, 0.0, float(BAND - 8 - WIN))
    tilt_lane = jnp.minimum(lax.broadcasted_iota(jnp.int32, (32, 128), 1), TILTS - 1)
    starts_v[...] = tilt_lane * BAND + local.astype(jnp.int32)
    to_smem = pltpu.make_async_copy(starts_v, starts_s, sem2)
    to_smem.start()
    offset = coord - (base + local)
    both = jnp.concatenate([jnp.broadcast_to(cosine, (8, 128)), jnp.broadcast_to(sine, (8, 128))], axis=0)
    for g in range(LANES // 128):
        lanes = slice(g * 128, (g + 1) * 128)
        which = jnp.broadcast_to(lane_tilt[0:1, lanes], (32, 128))
        cst[:, lanes] = jnp.take_along_axis(offset, which, axis=1) - lane_pixel[0:1, lanes]
        trig[:, lanes] = jnp.take_along_axis(both, which[0:16], axis=1)

    batch = 16

    def turn(group, carry):
        wide = []
        for b in range(batch):
            for step in range(3):
                piece = scr[pl.ds(group * size + b * 3 + step, BLOCKS, stride=ROWS_MSG), :]
                wide += [jnp.where(low, piece, 0.0).astype(BF), jnp.where(low, 0.0, piece).astype(BF)]
        turned = dot_t(fold, jnp.concatenate(wide, axis=0))
        for i in range(3 * batch):
            at = pl.multiple_of(group * (batch * BAND) + i * EDGE, EDGE)
            win[pl.ds(at, EDGE), :] = turned[:, i * 128 : (i + 1) * 128]
        return carry

    lax.fori_loop(0, 4, turn, 0)
    to_smem.wait()

    zcol = lax.broadcasted_iota(jnp.int32, (TILE, 256), 0).astype(F32)

    def tile(number, carry):
        right = jnp.concatenate(
            [win[pl.ds(starts_s[number, i], WIN), :] for i in range(TILTS)], axis=0
        ).astype(BF)
        total = jnp.zeros((TILE * TILE, 128), F32)
        for chunk in range(LANES // 256):
            lanes = slice(chunk * 256, (chunk + 1) * 256)
            cos_l = trig[0:1, lanes]
            here = zcol * trig[8:9, lanes] + cst[pl.ds(number, 1), lanes]
            pieces = []
            for _ in range(TILE):
                pieces.append(jnp.maximum(1.0 - jnp.abs(here), 0.0).astype(BF))
                here = here + cos_l
            total = total + dot(jnp.concatenate(pieces, axis=0), right[lanes])
        rounded = total.astype(BF)
        xt, zt = number // 8, lax.rem(number, 8)
        for i in range(TILE):
            at = pl.multiple_of((xt * TILE + i) * DEPTH + zt * TILE, TILE)
            part[pl.ds(at, TILE), :] = rounded[i * TILE : (i + 1) * TILE]
        return carry

    lax.fori_loop(0, 32, tile, 0)


def mate_kernel(x_ref, o_ref, send, recv):
    v = lax.axis_index("vol")
    t = lax.axis_index("tilt")
    mate = (t // 2) * 2 + (1 - lax.rem(t, 2))
    barrier = pltpu.get_barrier_semaphore()
    pl.semaphore_signal(barrier, inc=1, device_id=(v, mate), device_id_type=MESH)
    pl.semaphore_wait(barrier, 1)
    there = pltpu.make_async_remote_copy(
        x_ref, o_ref, send, recv, device_id=(v, mate), device_id_type=MESH
    )
    there.start()
    there.wait()


def box_kernel(own_ref, other_ref, corner_ref, owner_ref, box_out, vol_out, land, ext, lines, box_ref, vol_ref, sem, out_sem):
    v = lax.axis_index("vol")
    t = lax.axis_index("tilt")
    core = lax.rem(t, 2)
    half = CELLS // 2
    arrive = [
        pltpu.make_async_copy(own_ref, land.at[core], sem.at[0]),
        pltpu.make_async_copy(other_ref, land.at[1 - core], sem.at[1]),
    ]
    for copy in arrive:
        copy.start()
    picks = owner_ref.shape[0]
    owners = [owner_ref[r, 0] for r in range(picks)]
    ranks = [sum([(owners[q] == owners[r]).astype(jnp.int32) for q in range(r)], jnp.int32(0)) for r in range(picks)]
    lane = lax.broadcasted_iota(jnp.int32, (BOX, 128), 1)
    y_of = (lane & 63) * 2 + (lane >> 6)
    line = lax.broadcasted_iota(jnp.int32, (BOX, 128), 0)
    quarter = (y_of == line + t * 32).astype(F32).astype(BF)[0:32]
    for copy in arrive:
        copy.wait()

    def slab(i, carry):
        rows = land[0, pl.ds(pl.multiple_of(i * 1024, 1024), 1024), :]
        both = dot_t(quarter, rows)
        for j in range(8):
            lines[pl.ds(i * 8 + j, 32, stride=COLS), :] = both[:, j * 128 : (j + 1) * 128]
        return carry

    lax.fori_loop(0, COLS // 8, slab, 0, unroll=2)
    for i in range(32):
        vol_ref[i] = lines[i * COLS : (i + 1) * COLS, :].astype(BF)
    copies = [pltpu.make_async_copy(vol_ref, vol_out, out_sem.at[4])]
    copies[0].start()
    for side in range(2):
        for i in range(8):
            ext[side * half + i * 1024 : side * half + (i + 1) * 1024, :] = land[
                side, i * 1024 : (i + 1) * 1024
            ].astype(F32)

    for slot in range(4):
        mine = [((owners[r] == t) & (ranks[r] == slot)).astype(jnp.int32) for r in range(picks)]
        present = sum(mine)
        x0 = sum([mine[r] * (corner_ref[0, r] - v * COLS) for r in range(picks)])
        y0 = sum([mine[r] * corner_ref[1, r] for r in range(picks)])
        z0 = sum([mine[r] * corner_ref[2, r] for r in range(picks)])
        chosen = ((y_of == line + y0) & (present > 0)).astype(F32).astype(BF)
        origin = x0 * DEPTH + z0

        def cut(i, carry):
            rows = jnp.concatenate(
                [ext[pl.ds(origin + (i * 8 + j) * DEPTH, BOX), :] for j in range(8)], axis=0
            ).astype(BF)
            box_ref[slot, :, pl.ds(pl.multiple_of(i * 512, 512), 512)] = dot_t(chosen, rows).astype(BF)
            return carry

        lax.fori_loop(0, BOX // 8, cut, 0, unroll=2)
        copies.append(pltpu.make_async_copy(box_ref.at[slot], box_out.at[slot], out_sem.at[slot]))
        copies[-1].start()
    for copy in copies:
        copy.wait()


def trig_of(tenths):
    angle = tenths.astype(F32) * (math.pi / 1800.0)
    return jnp.cos(angle), jnp.sin(angle)


def per_device(images, angle_tenths, dose_index, box_corner, box_owner):
    vm = pl.BlockSpec(memory_space=pltpu.VMEM)
    sm = pl.BlockSpec(memory_space=pltpu.SMEM)
    anym = pl.BlockSpec(memory_space=pl.ANY)
    dma = pltpu.SemaphoreType.DMA
    tables = [jnp.asarray(a) for a in fft_tables()]
    recv = pl.pallas_call(
        exchange_kernel,
        out_shape=jax.ShapeDtypeStruct((4, BLOCKS, ROWS_MSG, 128), BF),
        in_specs=[vm] * 6 + [sm] * 2,
        out_specs=anym,
        scratch_shapes=[
            pltpu.VMEM((32 * 32, 128), F32),
            pltpu.VMEM((BLOCKS * ROWS_MSG, 128), F32),
            pltpu.VMEM((BLOCKS, ROWS_MSG, 128), BF),
            dma, dma, dma((2, 8)), dma, dma((2, 8)), dma, dma((2, 2, 8)),
        ],
        compiler_params=pltpu.CompilerParams(
            vmem_limit_bytes=VMEM_LIMIT, collective_id=1, has_side_effects=True
        ),
        name="exchange",
    )(images, *tables, angle_tenths.reshape(1, TILTS_HERE), angle_tenths, dose_index)

    lanes = np.arange(LANES)
    lane_tilt = jnp.asarray(np.broadcast_to(lanes // WIN, (8, LANES)).astype(np.int32))
    lane_pixel = jnp.asarray(np.broadcast_to(lanes % WIN, (8, LANES)).astype(np.float32))
    part = pl.pallas_call(
        project_kernel,
        out_shape=jax.ShapeDtypeStruct((CELLS // 2, 128), BF),
        in_specs=[anym, vm, vm],
        out_specs=vm,
        scratch_shapes=[
            pltpu.VMEM((4, BLOCKS, ROWS_MSG, 128), BF),
            pltpu.VMEM((4 * BLOCKS * ROWS_MSG, 128), F32),
            pltpu.VMEM((TILTS * BAND, 128), F32),
            pltpu.VMEM((32, 128), jnp.int32),
            pltpu.SMEM((32, 128), jnp.int32),
            pltpu.VMEM((32, LANES), F32),
            pltpu.VMEM((16, LANES), F32),
            dma((4,)),
            dma,
        ],
        compiler_params=pltpu.CompilerParams(vmem_limit_bytes=VMEM_LIMIT),
        name="project",
    )(recv, lane_tilt, lane_pixel)

    other = pl.pallas_call(
        mate_kernel,
        out_shape=jax.ShapeDtypeStruct((CELLS // 2, 128), BF),
        in_specs=[anym],
        out_specs=anym,
        scratch_shapes=[dma, dma],
        compiler_params=pltpu.CompilerParams(collective_id=2, has_side_effects=True),
        name="mate",
    )(part)

    boxes, volume = pl.pallas_call(
        box_kernel,
        out_shape=(
            jax.ShapeDtypeStruct((4, BOX, BOX * BOX), BF),
            jax.ShapeDtypeStruct((32, COLS, DEPTH), BF),
        ),
        in_specs=[anym, anym, sm, sm],
        out_specs=(anym, anym),
        scratch_shapes=[
            pltpu.VMEM((2, CELLS // 2, 128), BF),
            pltpu.VMEM((CELLS, 128), F32),
            pltpu.VMEM((32 * COLS, 128), F32),
            pltpu.VMEM((4, BOX, BOX * BOX), BF),
            pltpu.VMEM((32, COLS, DEPTH), BF),
            dma((2,)),
            dma((5,)),
        ],
        compiler_params=pltpu.CompilerParams(vmem_limit_bytes=VMEM_LIMIT),
        name="boxes",
    )(part, other, box_corner, box_owner)
    return volume, boxes.reshape(1, 1, 4, BOX, BOX * BOX)


def solution(mesh):
    in_specs = (P("tilt", "vol", None), P("tilt"), P("tilt"), P(None, "vol"), P("vol", None))
    out_specs = (P("tilt", "vol", None), P("vol", "tilt", None, None, None))
    return jax.shard_map(
        per_device, mesh=mesh, in_specs=in_specs, out_specs=out_specs, check_vma=False
    )
```

```python
import functools
import math

import jax
import jax.numpy as jnp
import ml_dtypes
import numpy as np
from jax import lax
from jax.experimental import pallas as pl
from jax.experimental.pallas import tpu as pltpu
from jax.sharding import PartitionSpec as P

MESH = pl.DeviceIdType.MESH
BF = jnp.bfloat16
F32 = jnp.float32

PIX = 4096
EDGE = 64
COLS = 64
DEPTH = 128
BOX = 64
BLOCKS = 64
TILTS_HERE = 16
TILTS = 64
ROWS_MSG = 48
BAND = 192
TILE = 16
WIN = 24
LANES = TILTS * WIN
CELLS = 2 * COLS * DEPTH

VMEM_LIMIT = 56 * 1024 * 1024


def split_np(table):
    high = table.astype(np.float32).astype(ml_dtypes.bfloat16)
    low = (table - high.astype(np.float64)).astype(np.float32).astype(ml_dtypes.bfloat16)
    return high, low


def fft_tables():
    grid = np.outer(np.arange(EDGE), np.arange(EDGE))
    cos_t = np.cos(2 * np.pi * (grid % EDGE) / EDGE)
    sin_t = np.sin(2 * np.pi * (grid % EDGE) / EDGE)
    stacked = np.concatenate([cos_t, sin_t], axis=0)
    s_hi, s_lo = split_np(stacked)
    left = np.concatenate([s_hi, s_lo], axis=0)
    order = np.concatenate([np.arange(0, EDGE, 2), np.arange(1, EDGE, 2)])
    left = np.stack([left[:, order], left])
    two = np.eye(2)
    cos2, sin2 = np.kron(two, cos_t), np.kron(two, sin_t)
    fwd = np.block([[cos2, -sin2], [sin2, cos2]])
    inv = np.block([[cos2, sin2], [-sin2, cos2]])
    f_hi, f_lo = split_np(fwd)
    i_hi, i_lo = split_np(inv)
    right = np.stack([f_hi, f_lo, i_hi, i_lo])
    twist = np.stack([np.cos(2 * np.pi * grid / PIX), np.sin(2 * np.pi * grid / PIX)])
    twist = np.concatenate([twist, twist], axis=2).astype(np.float32)
    k1, k2 = np.meshgrid(np.arange(EDGE), np.arange(EDGE), indexing="ij")
    freq = k1 + EDGE * k2
    freq = np.minimum(freq, PIX - freq)
    ratio = 2.0 * freq / PIX
    bend = ratio * np.sqrt(ratio)
    ramp = np.where(freq * 2 == PIX, 0.0, freq / PIX) / PIX
    shape = np.stack([bend, ramp])
    shape = np.concatenate([shape, shape], axis=2).astype(np.float32)
    return left, right, twist, shape


def dot(a, b):
    return jnp.dot(a, b, preferred_element_type=F32)


def dot_t(a, b):
    return lax.dot_general(a, b, (((1,), (1,)), ((), ())), preferred_element_type=F32)


def halves(value):
    high = value.astype(BF)
    return high, (value - high.astype(F32)).astype(BF)


def filter_pairs(pairs, x_ref, left_ref, right_ref, twist_ref, shape_ref, angle_row, angle_ref, dose_ref, cube, scr):
    first_left, left = left_ref[0], left_ref[1]
    cos_w, sin_w = twist_ref[0], twist_ref[1]
    bend, ramp = shape_ref[0], shape_ref[1]
    lane = lax.broadcasted_iota(jnp.int32, (EDGE, 128), 1)
    first = lane < EDGE
    thin = first[0:32]
    n1 = lax.broadcasted_iota(jnp.int32, (BLOCKS, EDGE), 1)
    cosine, sine = trig_of(angle_row[...])
    columns = lax.broadcasted_iota(jnp.int32, (BLOCKS, TILTS_HERE), 0).astype(F32) * COLS
    lowest = (
        PIX / 2
        + (columns - PIX / 2) * cosine
        + jnp.minimum(-(DEPTH / 2) * sine, (DEPTH / 2 - 1) * sine)
    )
    begin = jnp.floor(lowest).astype(jnp.int32) - 1
    quots, rests = begin >> 6, begin & 63

    def side(row, pair):
        one = cube[pl.ds((pair * 4 + row) * 32, 32), :]
        two = cube[pl.ds((pair * 4 + 2 + row) * 32, 32), :]
        even = jnp.where(thin, one, pltpu.roll(two, EDGE, 1))
        odd = jnp.where(thin, pltpu.roll(one, EDGE, 1), two)
        return jnp.concatenate([even, odd], axis=0).astype(BF)

    for pair in pairs:
        part = dot(first_left, jnp.concatenate([side(0, pair), side(1, pair)], axis=1))
        cx = part[0:64] + part[128:192]
        sx = part[64:128] + part[192:256]
        re = cx[:, :128] + sx[:, 128:]
        im = cx[:, 128:] - sx[:, :128]
        turned = jnp.concatenate([re * cos_w + im * sin_w, im * cos_w - re * sin_w], axis=1)
        hi, lo = halves(turned)
        spec = dot(hi, right_ref[0]) + (dot(lo, right_ref[0]) + dot(hi, right_ref[1]))
        dose = jnp.where(first, dose_ref[2 * pair].astype(F32), dose_ref[2 * pair + 1].astype(F32))
        resp = ramp * jnp.exp((-0.05 * dose) * bend)
        spec = spec * jnp.concatenate([resp, resp], axis=1)
        hi, lo = halves(spec)
        back = dot(hi, right_ref[2]) + (dot(lo, right_ref[2]) + dot(hi, right_ref[3]))
        re, im = back[:, :128], back[:, 128:]
        turned = jnp.concatenate([re * cos_w - im * sin_w, im * cos_w + re * sin_w], axis=1)
        hi, lo = halves(turned)
        part = dot(left, hi)
        extra = dot(left[0:128], lo)
        cx = part[0:64] + (part[128:192] + extra[0:64])
        sx = part[64:128] + (part[192:256] + extra[64:128])
        re = cx[:, :128] - sx[:, 128:]
        im = cx[:, 128:] + sx[:, :128]
        rows = (
            jnp.where(first, re, pltpu.roll(im, EDGE, 1)),
            jnp.where(first, pltpu.roll(re, EDGE, 1), im),
        )
        for half in range(2):
            tilt = 2 * pair + half
            image = rows[half].astype(BF)
            quot = quots[:, tilt : tilt + 1]
            rest = rests[:, tilt : tilt + 1]
            pick = jnp.concatenate(
                [(n1 == quot + step).astype(F32).astype(BF) for step in range(4)], axis=0
            )
            near = dot(pick, image)
            at = (lane & EDGE) | ((lane + rest) & (EDGE - 1))
            stay = (lane & (EDGE - 1)) + rest < EDGE
            moved = [
                jnp.take_along_axis(near[step * EDGE : (step + 1) * EDGE], at, axis=1)
                for step in range(4)
            ]
            for step in range(3):
                piece = jnp.where(stay, moved[step], moved[step + 1])
                if step == 2:
                    tenths = angle_ref[tilt]
                    piece = jnp.where(lane == 60, (tenths >> 5).astype(F32), piece)
                    piece = jnp.where(lane == 61, (tenths & 31).astype(F32), piece)
                    piece = jnp.where(lane == 62, quot.astype(F32), piece)
                    piece = jnp.where(lane == 63, rest.astype(F32), piece)
                scr[pl.ds(tilt * 3 + step, BLOCKS, stride=ROWS_MSG), :] = piece


def exchange_kernel(
    image_ref, left_ref, right_ref, twist_ref, shape_ref, angle_row, angle_ref, dose_ref, o_ref,
    cube, scr, x_ref, loc_sem, a_send, a_recv, x_send, x_recv, m_send, m_recv,
):
    v = lax.axis_index("vol")
    t = lax.axis_index("tilt")
    y, z, xh = lax.rem(v, 4), lax.rem(v // 4, 8), v // 32
    core, xl = lax.rem(t, 2), t // 2
    mate = xl * 2 + (1 - core)
    cross = (1 - xl) * 2 + core
    barrier = pltpu.get_barrier_semaphore()

    def greet(i, carry):
        p = lax.rem(xh * 32 + i, 64)
        q = jnp.where(i < 32, t, cross)

        @pl.when(p != v)
        def _():
            pl.semaphore_signal(barrier, inc=1, device_id=(p, q), device_id_type=MESH)

        return carry

    lax.fori_loop(0, 64, greet, 0)
    pl.semaphore_signal(barrier, inc=1, device_id=(v, cross), device_id_type=MESH)
    pl.semaphore_signal(barrier, inc=1, device_id=(v, mate), device_id_type=MESH)

    for tilt in range(TILTS_HERE):
        wide = image_ref[tilt].astype(F32)
        for j in range(PIX // 128):
            cube[pl.ds(tilt * 64 + j, 2, stride=32), :] = wide[:, j * 128 : (j + 1) * 128]

    operands = (image_ref, left_ref, right_ref, twist_ref, shape_ref, angle_row, angle_ref, dose_ref, cube, scr)
    steps = (0, 1, 7, 2, 6, 3, 5, 4)

    def send_rows(low, high):
        for block in range(BLOCKS):
            x_ref[block, low:high] = scr[block * ROWS_MSG + low : block * ROWS_MSG + high, :].astype(BF)
        for dz in steps:
            for far in range(2):
                for dy in range(4):
                    if dz == 0 and far == 0 and dy == 0:
                        continue
                    zz, yy = lax.rem(z + dz, 8), lax.rem(y + dy, 4)
                    p = (xh if far == 0 else 1 - xh) * 32 + zz * 4 + yy
                    pltpu.make_async_remote_copy(
                        x_ref.at[p, pl.ds(low, high - low)],
                        o_ref.at[t, v, pl.ds(low, high - low)],
                        a_send,
                        a_recv.at[far, z],
                        device_id=(p, t if far == 0 else cross),
                        device_id_type=MESH,
                    ).start()

    filter_pairs(range(0, 3), *operands)
    pl.semaphore_wait(barrier, 65)
    send_rows(0, 16)
    filter_pairs(range(3, 8), *operands)
    send_rows(16, 48)
    own = pltpu.make_async_copy(x_ref.at[v], o_ref.at[t, v], loc_sem)
    own.start()
    for dz in steps:
        for far in range(2):
            zz = lax.rem(z + 8 - dz, 8)
            base = (xh if far == 0 else 1 - xh) * 32 + zz * 4
            slot = t if far == 0 else cross
            number = 4
            if dz == 0 and far == 0:
                own.wait()
                number = 3
            pltpu.make_async_copy(
                o_ref.at[slot, pl.ds(base, number)], o_ref.at[slot, pl.ds(base, number)], a_recv.at[far, zz]
            ).wait()
            block = o_ref.at[slot, pl.ds(base, 4)]
            pltpu.make_async_remote_copy(
                block, block, x_send, x_recv.at[far, zz], device_id=(v, cross), device_id_type=MESH
            ).start()
            pltpu.make_async_remote_copy(
                block, block, m_send, m_recv.at[0, far, zz], device_id=(v, mate), device_id_type=MESH
            ).start()
    for dz in steps:
        for far in range(2):
            zz = lax.rem(z + 8 - dz, 8)
            base = (xh if far == 0 else 1 - xh) * 32 + zz * 4
            slot = cross if far == 0 else t
            block = o_ref.at[slot, pl.ds(base, 4)]
            pltpu.make_async_copy(block, block, x_recv.at[far, zz]).wait()
            pltpu.make_async_remote_copy(
                block, block, m_send, m_recv.at[1, far, zz], device_id=(v, mate), device_id_type=MESH
            ).start()
    mate_cross = (1 - xl) * 2 + (1 - core)
    for kind in range(2):
        for far in range(2):
            for zz in range(8):
                base = (xh if far == 0 else 1 - xh) * 32 + zz * 4
                slot = mate if (kind + far) % 2 == 0 else mate_cross
                block = o_ref.at[slot, pl.ds(base, 4)]
                pltpu.make_async_copy(block, block, m_recv.at[kind, far, zz]).wait()
    pltpu.make_async_copy(x_ref.at[pl.ds(0, 63)], x_ref.at[pl.ds(0, 63)], a_send).wait()
    half = o_ref.at[0]
    pltpu.make_async_copy(half, half, x_send).wait()
    both = o_ref.at[pl.ds(0, 2)]
    pltpu.make_async_copy(both, both, m_send).wait()


def project_kernel(
    recv_ref, lane_tilt, lane_pixel, own_ref, other_ref,
    land, scr, win, starts_v, starts_s, cst, trig, part, sem, sem2, loc, send, recv,
):
    v = lax.axis_index("vol")
    t = lax.axis_index("tilt")
    core = lax.rem(t, 2)
    mate = (t // 2) * 2 + (1 - core)
    barrier = pltpu.get_barrier_semaphore()
    pl.semaphore_signal(barrier, inc=1, device_id=(v, mate), device_id_type=MESH)
    size = BLOCKS * ROWS_MSG
    arrive = [pltpu.make_async_copy(recv_ref.at[g], land.at[g], sem.at[g]) for g in range(4)]
    for copy in arrive:
        copy.start()
    lane = lax.broadcasted_iota(jnp.int32, (BLOCKS, 128), 1)
    low = lane < EDGE
    fold = (
        lax.broadcasted_iota(jnp.int32, (EDGE, 128), 0) == (lane & (EDGE - 1))
    ).astype(F32).astype(BF)
    for group in range(4):
        arrive[group].wait()
        scr[group * size : (group + 1) * size, :] = land[group].reshape(size, 128).astype(F32)

    heads = [scr[pl.ds(g * size + 2, TILTS_HERE, stride=3), :] for g in range(4)]
    heads = jnp.concatenate(heads + [jnp.zeros((128 - TILTS, 128), F32)], axis=0).T
    tenths = heads[60:61] * 32.0 + heads[61:62]
    base = heads[62:63] * 64.0 + heads[63:64]
    cosine, sine = trig_of(tenths)
    number = lax.broadcasted_iota(jnp.int32, (32, 128), 0)
    x_tile = ((number >> 3) * TILE + (v + core) * COLS).astype(F32)
    z_tile = ((number & 7) * TILE).astype(F32)
    coord = PIX / 2 + (x_tile - PIX / 2) * cosine + (z_tile - DEPTH / 2) * sine
    local = jnp.floor(coord + jnp.minimum((TILE - 1) * sine, 0.0)) - base
    local = jnp.clip(local.astype(jnp.int32), 0, BAND - 8 - WIN)
    tilt_lane = jnp.minimum(lax.broadcasted_iota(jnp.int32, (32, 128), 1), TILTS - 1)
    starts_v[...] = tilt_lane * BAND + local
    to_smem = pltpu.make_async_copy(starts_v, starts_s, sem2)
    to_smem.start()
    offset = coord - (base + local.astype(F32))
    both = jnp.concatenate([jnp.broadcast_to(cosine, (8, 128)), jnp.broadcast_to(sine, (8, 128))], axis=0)
    for g in range(LANES // 128):
        lanes = slice(g * 128, (g + 1) * 128)
        which = jnp.broadcast_to(lane_tilt[0:1, lanes], (32, 128))
        cst[:, lanes] = jnp.take_along_axis(offset, which, axis=1) - lane_pixel[0:1, lanes]
        trig[:, lanes] = jnp.take_along_axis(both, which[0:16], axis=1)

    batch = 16

    def turn(group, carry):
        wide = []
        for b in range(batch):
            for step in range(3):
                piece = scr[pl.ds(group * size + b * 3 + step, BLOCKS, stride=ROWS_MSG), :]
                wide += [jnp.where(low, piece, 0.0).astype(BF), jnp.where(low, 0.0, piece).astype(BF)]
        turned = dot_t(fold, jnp.concatenate(wide, axis=0))
        for i in range(3 * batch):
            at = pl.multiple_of(group * (batch * BAND) + i * EDGE, EDGE)
            win[pl.ds(at, EDGE), :] = turned[:, i * 128 : (i + 1) * 128]
        return carry

    lax.fori_loop(0, 4, turn, 0)
    to_smem.wait()

    zcol = lax.broadcasted_iota(jnp.int32, (TILE, 256), 0).astype(F32)

    def tile(number, carry):
        right = jnp.concatenate(
            [win[pl.ds(starts_s[number, i], WIN), :] for i in range(TILTS)], axis=0
        ).astype(BF)
        total = jnp.zeros((TILE * TILE, 128), F32)
        for chunk in range(LANES // 256):
            lanes = slice(chunk * 256, (chunk + 1) * 256)
            cos_l = trig[0:1, lanes]
            here = zcol * trig[8:9, lanes] + cst[pl.ds(number, 1), lanes]
            pieces = []
            for _ in range(TILE):
                pieces.append(jnp.maximum(1.0 - jnp.abs(here), 0.0).astype(BF))
                here = here + cos_l
            total = total + dot(jnp.concatenate(pieces, axis=0), right[lanes])
        rounded = total.astype(BF)
        xt, zt = number // 8, lax.rem(number, 8)
        for i in range(TILE):
            at = pl.multiple_of((xt * TILE + i) * DEPTH + zt * TILE, TILE)
            part[pl.ds(at, TILE), :] = rounded[i * TILE : (i + 1) * TILE]
        return carry

    span = TILE * DEPTH
    copies = []
    for xt in range(4):
        lax.fori_loop(8 * xt, 8 * xt + 8, tile, 0)
        if xt == 0:
            pl.semaphore_wait(barrier, 1)
        slab = pl.ds(xt * span, span)
        there = pltpu.make_async_remote_copy(
            part.at[slab], other_ref.at[slab], send.at[xt], recv.at[xt],
            device_id=(v, mate), device_id_type=MESH,
        )
        here = pltpu.make_async_copy(part.at[slab], own_ref.at[slab], loc.at[xt])
        there.start()
        here.start()
        copies += [there, here]
    for copy in copies:
        copy.wait()


def box_kernel(own_ref, other_ref, corner_ref, owner_ref, box_out, vol_out, land, ext, lines, box_ref, vol_ref, sem, out_sem):
    v = lax.axis_index("vol")
    t = lax.axis_index("tilt")
    core = lax.rem(t, 2)
    half = CELLS // 2
    arrive = [
        pltpu.make_async_copy(own_ref, land.at[core], sem.at[0]),
        pltpu.make_async_copy(other_ref, land.at[1 - core], sem.at[1]),
    ]
    for copy in arrive:
        copy.start()
    picks = owner_ref.shape[1]
    owners = [owner_ref[0, r] for r in range(picks)]
    ranks = [sum([(owners[q] == owners[r]).astype(jnp.int32) for q in range(r)], jnp.int32(0)) for r in range(picks)]
    lane = lax.broadcasted_iota(jnp.int32, (BOX, 128), 1)
    y_of = (lane & 63) * 2 + (lane >> 6)
    line = lax.broadcasted_iota(jnp.int32, (BOX, 128), 0)
    quarter = (y_of == line + t * 32).astype(F32).astype(BF)[0:32]
    for copy in arrive:
        copy.wait()

    def slab(i, carry):
        rows = land[0, pl.ds(pl.multiple_of(i * 1024, 1024), 1024), :]
        both = dot_t(quarter, rows)
        for j in range(8):
            lines[pl.ds(i * 8 + j, 32, stride=COLS), :] = both[:, j * 128 : (j + 1) * 128]
        return carry

    lax.fori_loop(0, COLS // 8, slab, 0, unroll=2)
    for i in range(32):
        vol_ref[i] = lines[i * COLS : (i + 1) * COLS, :].astype(BF)
    copies = [pltpu.make_async_copy(vol_ref, vol_out, out_sem.at[4])]
    copies[0].start()
    for side in range(2):
        for i in range(8):
            ext[side * half + i * 1024 : side * half + (i + 1) * 1024, :] = land[
                side, i * 1024 : (i + 1) * 1024
            ].astype(F32)

    for slot in range(4):
        mine = [((owners[r] == t) & (ranks[r] == slot)).astype(jnp.int32) for r in range(picks)]
        present = sum(mine)
        x0 = sum([mine[r] * (corner_ref[0, r] - v * COLS) for r in range(picks)])
        y0 = sum([mine[r] * corner_ref[1, r] for r in range(picks)])
        z0 = sum([mine[r] * corner_ref[2, r] for r in range(picks)])
        chosen = ((y_of == line + y0) & (present > 0)).astype(F32).astype(BF)
        origin = x0 * DEPTH + z0

        def cut(i, carry):
            rows = jnp.concatenate(
                [ext[pl.ds(origin + (i * 8 + j) * DEPTH, BOX), :] for j in range(8)], axis=0
            ).astype(BF)
            box_ref[slot, :, pl.ds(pl.multiple_of(i * 512, 512), 512)] = dot_t(chosen, rows).astype(BF)
            return carry

        lax.fori_loop(0, BOX // 8, cut, 0, unroll=2)
        copies.append(pltpu.make_async_copy(box_ref.at[slot], box_out.at[slot], out_sem.at[slot]))
        copies[-1].start()
    for copy in copies:
        copy.wait()


def trig_of(tenths):
    angle = tenths.astype(F32) * (math.pi / 1800.0)
    return jnp.cos(angle), jnp.sin(angle)


def per_device(images, angle_tenths, dose_index, box_corner, box_owner):
    vm = pl.BlockSpec(memory_space=pltpu.VMEM)
    sm = pl.BlockSpec(memory_space=pltpu.SMEM)
    anym = pl.BlockSpec(memory_space=pl.ANY)
    dma = pltpu.SemaphoreType.DMA
    tables = [jnp.asarray(a) for a in fft_tables()]
    recv = pl.pallas_call(
        exchange_kernel,
        out_shape=jax.ShapeDtypeStruct((4, BLOCKS, ROWS_MSG, 128), BF),
        in_specs=[vm] * 6 + [sm] * 2,
        out_specs=anym,
        scratch_shapes=[
            pltpu.VMEM((32 * 32, 128), F32),
            pltpu.VMEM((BLOCKS * ROWS_MSG, 128), F32),
            pltpu.VMEM((BLOCKS, ROWS_MSG, 128), BF),
            dma, dma, dma((2, 8)), dma, dma((2, 8)), dma, dma((2, 2, 8)),
        ],
        compiler_params=pltpu.CompilerParams(
            vmem_limit_bytes=VMEM_LIMIT, collective_id=1, has_side_effects=True
        ),
        name="exchange",
    )(images, *tables, angle_tenths.reshape(1, TILTS_HERE), angle_tenths, dose_index)

    lanes = np.arange(LANES)
    lane_tilt = jnp.asarray(np.broadcast_to(lanes // WIN, (8, LANES)).astype(np.int32))
    lane_pixel = jnp.asarray(np.broadcast_to(lanes % WIN, (8, LANES)).astype(np.float32))
    part, other = pl.pallas_call(
        project_kernel,
        out_shape=(jax.ShapeDtypeStruct((CELLS // 2, 128), BF),) * 2,
        in_specs=[anym, vm, vm],
        out_specs=(anym, anym),
        scratch_shapes=[
            pltpu.VMEM((4, BLOCKS, ROWS_MSG, 128), BF),
            pltpu.VMEM((4 * BLOCKS * ROWS_MSG, 128), F32),
            pltpu.VMEM((TILTS * BAND, 128), F32),
            pltpu.VMEM((32, 128), jnp.int32),
            pltpu.SMEM((32, 128), jnp.int32),
            pltpu.VMEM((32, LANES), F32),
            pltpu.VMEM((16, LANES), F32),
            pltpu.VMEM((CELLS // 2, 128), BF),
            dma((4,)),
            dma,
            dma((4,)),
            dma((4,)),
            dma((4,)),
        ],
        compiler_params=pltpu.CompilerParams(
            vmem_limit_bytes=VMEM_LIMIT, collective_id=2, has_side_effects=True
        ),
        name="project",
    )(recv, lane_tilt, lane_pixel)

    boxes, volume = pl.pallas_call(
        box_kernel,
        out_shape=(
            jax.ShapeDtypeStruct((4, BOX, BOX * BOX), BF),
            jax.ShapeDtypeStruct((32, COLS, DEPTH), BF),
        ),
        in_specs=[anym, anym, sm, sm],
        out_specs=(anym, anym),
        scratch_shapes=[
            pltpu.VMEM((2, CELLS // 2, 128), BF),
            pltpu.VMEM((CELLS, 128), F32),
            pltpu.VMEM((32 * COLS, 128), F32),
            pltpu.VMEM((4, BOX, BOX * BOX), BF),
            pltpu.VMEM((32, COLS, DEPTH), BF),
            dma((2,)),
            dma((5,)),
        ],
        compiler_params=pltpu.CompilerParams(vmem_limit_bytes=VMEM_LIMIT),
        name="boxes",
    )(part, other, box_corner, box_owner.T)
    return volume, boxes.reshape(1, 1, 4, BOX, BOX * BOX)


def solution(mesh):
    in_specs = (P("tilt", "vol", None), P("tilt"), P("tilt"), P(None, "vol"), P("vol", None))
    out_specs = (P("tilt", "vol", None), P("vol", "tilt", None, None, None))
    return jax.shard_map(
        per_device, mesh=mesh, in_specs=in_specs, out_specs=out_specs, check_vma=False
    )
```

```python
import functools
import math

import jax
import jax.numpy as jnp
import ml_dtypes
import numpy as np
from jax import lax
from jax.experimental import pallas as pl
from jax.experimental.pallas import tpu as pltpu
from jax.sharding import PartitionSpec as P

MESH = pl.DeviceIdType.MESH
BF = jnp.bfloat16
F32 = jnp.float32

PIX = 4096
EDGE = 64
COLS = 64
DEPTH = 128
BOX = 64
BLOCKS = 64
TILTS_HERE = 16
TILTS = 64
BAND = 192
TILE = 16
WIN = 24
STAGE_ROWS = 16
SPLIT = 5
STAGE_TILTS = ((0, 1, 2, 3, 4), (6, 7, 8, 9, 10), (11, 12, 13, 14, 15, SPLIT))
STAGE_CHUNKS = ((256, 256), (256, 256), (256, 256, 128))
STAGE_LANES = (0, 512, 1024, 1792)
META = 56
CELLS = 2 * COLS * DEPTH

VMEM_LIMIT = 56 * 1024 * 1024


def split_np(table):
    high = table.astype(np.float32).astype(ml_dtypes.bfloat16)
    low = (table - high.astype(np.float64)).astype(np.float32).astype(ml_dtypes.bfloat16)
    return high, low


def fft_tables():
    grid = np.outer(np.arange(EDGE), np.arange(EDGE))
    cos_t = np.cos(2 * np.pi * (grid % EDGE) / EDGE)
    sin_t = np.sin(2 * np.pi * (grid % EDGE) / EDGE)
    stacked = np.concatenate([cos_t, sin_t], axis=0)
    s_hi, s_lo = split_np(stacked)
    left = np.concatenate([s_hi, s_lo], axis=0)
    order = np.concatenate([np.arange(0, EDGE, 2), np.arange(1, EDGE, 2)])
    left = np.stack([left[:, order], left])
    two = np.eye(2)
    cos2, sin2 = np.kron(two, cos_t), np.kron(two, sin_t)
    fwd = np.block([[cos2, -sin2], [sin2, cos2]])
    inv = np.block([[cos2, sin2], [-sin2, cos2]])
    f_hi, f_lo = split_np(fwd)
    i_hi, i_lo = split_np(inv)
    right = np.stack([f_hi, f_lo, i_hi, i_lo])
    twist = np.stack([np.cos(2 * np.pi * grid / PIX), np.sin(2 * np.pi * grid / PIX)])
    twist = np.concatenate([twist, twist], axis=2).astype(np.float32)
    k1, k2 = np.meshgrid(np.arange(EDGE), np.arange(EDGE), indexing="ij")
    freq = k1 + EDGE * k2
    freq = np.minimum(freq, PIX - freq)
    ratio = 2.0 * freq / PIX
    bend = ratio * np.sqrt(ratio)
    ramp = np.where(freq * 2 == PIX, 0.0, freq / PIX) / PIX
    shape = np.stack([bend, ramp])
    shape = np.concatenate([shape, shape], axis=2).astype(np.float32)
    return left, right, twist, shape


def dot(a, b):
    return jnp.dot(a, b, preferred_element_type=F32)


def dot_t(a, b):
    return lax.dot_general(a, b, (((1,), (1,)), ((), ())), preferred_element_type=F32)


def halves(value):
    high = value.astype(BF)
    return high, (value - high.astype(F32)).astype(BF)


def message_row(tilt, step):
    if tilt == SPLIT:
        return step, STAGE_ROWS - 1
    order = tilt - (tilt > SPLIT)
    return order // 5, 3 * (order % 5) + step


def filter_pairs(pairs, x_ref, left_ref, right_ref, twist_ref, shape_ref, angle_row, angle_ref, dose_ref, cube, scr):
    first_left, left = left_ref[0], left_ref[1]
    cos_w, sin_w = twist_ref[0], twist_ref[1]
    bend, ramp = shape_ref[0], shape_ref[1]
    lane = lax.broadcasted_iota(jnp.int32, (EDGE, 128), 1)
    first = lane < EDGE
    thin = first[0:32]
    n1 = lax.broadcasted_iota(jnp.int32, (BLOCKS, EDGE), 1)
    cosine, sine = trig_of(angle_row[...])
    columns = lax.broadcasted_iota(jnp.int32, (BLOCKS, TILTS_HERE), 0).astype(F32) * COLS
    lowest = (
        PIX / 2
        + (columns - PIX / 2) * cosine
        + jnp.minimum(-(DEPTH / 2) * sine, (DEPTH / 2 - 1) * sine)
    )
    begin = jnp.floor(lowest).astype(jnp.int32) - 1
    quots, rests = begin >> 6, begin & 63

    def side(row, pair):
        one = cube[pl.ds((pair * 4 + row) * 32, 32), :]
        two = cube[pl.ds((pair * 4 + 2 + row) * 32, 32), :]
        even = jnp.where(thin, one, pltpu.roll(two, EDGE, 1))
        odd = jnp.where(thin, pltpu.roll(one, EDGE, 1), two)
        return jnp.concatenate([even, odd], axis=0).astype(BF)

    for pair in pairs:
        part = dot(first_left, jnp.concatenate([side(0, pair), side(1, pair)], axis=1))
        cx = part[0:64] + part[128:192]
        sx = part[64:128] + part[192:256]
        re = cx[:, :128] + sx[:, 128:]
        im = cx[:, 128:] - sx[:, :128]
        turned = jnp.concatenate([re * cos_w + im * sin_w, im * cos_w - re * sin_w], axis=1)
        hi, lo = halves(turned)
        spec = dot(hi, right_ref[0]) + (dot(lo, right_ref[0]) + dot(hi, right_ref[1]))
        dose = jnp.where(first, dose_ref[2 * pair].astype(F32), dose_ref[2 * pair + 1].astype(F32))
        resp = ramp * jnp.exp((-0.05 * dose) * bend)
        spec = spec * jnp.concatenate([resp, resp], axis=1)
        hi, lo = halves(spec)
        back = dot(hi, right_ref[2]) + (dot(lo, right_ref[2]) + dot(hi, right_ref[3]))
        re, im = back[:, :128], back[:, 128:]
        turned = jnp.concatenate([re * cos_w - im * sin_w, im * cos_w + re * sin_w], axis=1)
        hi, lo = halves(turned)
        part = dot(left, hi)
        extra = dot(left[0:128], lo)
        cx = part[0:64] + (part[128:192] + extra[0:64])
        sx = part[64:128] + (part[192:256] + extra[64:128])
        re = cx[:, :128] - sx[:, 128:]
        im = cx[:, 128:] + sx[:, :128]
        rows = (
            jnp.where(first, re, pltpu.roll(im, EDGE, 1)),
            jnp.where(first, pltpu.roll(re, EDGE, 1), im),
        )
        for half in range(2):
            tilt = 2 * pair + half
            image = rows[half].astype(BF)
            quot = quots[:, tilt : tilt + 1]
            rest = rests[:, tilt : tilt + 1]
            pick = jnp.concatenate(
                [(n1 == quot + step).astype(F32).astype(BF) for step in range(4)], axis=0
            )
            near = dot(pick, image)
            at = (lane & EDGE) | ((lane + rest) & (EDGE - 1))
            stay = (lane & (EDGE - 1)) + rest < EDGE
            moved = [
                jnp.take_along_axis(near[step * EDGE : (step + 1) * EDGE], at, axis=1)
                for step in range(4)
            ]
            for step in range(3):
                piece = jnp.where(stay, moved[step], moved[step + 1])
                if step == 2 and tilt < 4:
                    for j in range(4):
                        other = 4 * tilt + j
                        tenths = angle_ref[other]
                        at_lane = META + 2 * j
                        piece = jnp.where(lane == at_lane, (tenths >> 5).astype(F32), piece)
                        piece = jnp.where(lane == at_lane + 1, (tenths & 31).astype(F32), piece)
                        quot_o = quots[:, other : other + 1].astype(F32)
                        rest_o = rests[:, other : other + 1].astype(F32)
                        piece = jnp.where(lane == at_lane + 64, quot_o, piece)
                        piece = jnp.where(lane == at_lane + 65, rest_o, piece)
                stage, row = message_row(tilt, step)
                scr[pl.ds(stage * BLOCKS * STAGE_ROWS + row, BLOCKS, stride=STAGE_ROWS), :] = piece


def main_kernel(
    image_ref, left_ref, right_ref, twist_ref, shape_ref, angle_row, angle_ref, dose_ref,
    lane_tilt, lane_pixel, own_ref, other_ref,
    cube, scr, x_ref, land, wide, win, acc, part, starts_v, starts_s, cst, trig,
    a_send, a_recv, x_send, x_recv, m_send, m_recv, sem2, loc, send, recv,
):
    v = lax.axis_index("vol")
    t = lax.axis_index("tilt")
    y, z, xh = lax.rem(v, 4), lax.rem(v // 4, 8), v // 32
    core, xl = lax.rem(t, 2), t // 2
    mate = xl * 2 + (1 - core)
    cross = (1 - xl) * 2 + core
    barrier = pltpu.get_barrier_semaphore()

    def greet(i, carry):
        p = lax.rem(xh * 32 + i, 64)
        q = jnp.where(i < 32, t, cross)

        @pl.when(p != v)
        def _():
            pl.semaphore_signal(barrier, inc=1, device_id=(p, q), device_id_type=MESH)

        return carry

    lax.fori_loop(0, 64, greet, 0)
    pl.semaphore_signal(barrier, inc=1, device_id=(v, cross), device_id_type=MESH)
    pl.semaphore_signal(barrier, inc=1, device_id=(v, mate), device_id_type=MESH)

    for tilt in range(TILTS_HERE):
        image = image_ref[tilt].astype(F32)
        for j in range(PIX // 128):
            cube[pl.ds(tilt * 64 + j, 2, stride=32), :] = image[:, j * 128 : (j + 1) * 128]

    operands = (image_ref, left_ref, right_ref, twist_ref, shape_ref, angle_row, angle_ref, dose_ref, cube, scr)
    steps = (0, 1, 7, 2, 6, 3, 5, 4)
    size = BLOCKS * STAGE_ROWS

    def send_stage(stage):
        x_ref[stage] = scr[stage * size : (stage + 1) * size, :].astype(BF).reshape(BLOCKS, STAGE_ROWS, 128)
        pltpu.make_async_copy(x_ref.at[stage, v], land.at[stage, t, v], a_recv.at[stage, 0, lax.div(z, 4)]).start()
        for dz in steps:
            for far in range(2):
                for dy in range(4):
                    if dz == 0 and far == 0 and dy == 0:
                        continue
                    zz, yy = lax.rem(z + dz, 8), lax.rem(y + dy, 4)
                    p = (xh if far == 0 else 1 - xh) * 32 + zz * 4 + yy
                    pltpu.make_async_remote_copy(
                        x_ref.at[stage, p],
                        land.at[stage, t, v],
                        a_send,
                        a_recv.at[stage, far, lax.div(z, 4)],
                        device_id=(p, t if far == 0 else cross),
                        device_id_type=MESH,
                    ).start()

    def chunk_of(i):
        far = lax.rem(i, 2)
        half = lax.rem(lax.div(z, 4) + lax.div(i, 2), 2)
        base = lax.rem(xh + far, 2) * 32 + half * 16
        near_slot = lax.rem(xl + far, 2) * 2 + core
        far_slot = lax.rem(xl + far + 1, 2) * 2 + core
        return far, half, base, near_slot, far_slot

    def pass_first(stage, i):
        far, zz, base, slot, _ = chunk_of(i)
        block = land.at[stage, slot, pl.ds(base, 16)]
        pltpu.make_async_copy(block, block, a_recv.at[stage, far, zz]).wait()
        pltpu.make_async_remote_copy(
            block, block, x_send, x_recv.at[stage, far, zz], device_id=(v, cross), device_id_type=MESH
        ).start()
        pltpu.make_async_remote_copy(
            block, block, m_send, m_recv.at[stage], device_id=(v, mate), device_id_type=MESH
        ).start()

    def pass_second(stage, i):
        far, zz, base, _, slot = chunk_of(i)
        block = land.at[stage, slot, pl.ds(base, 16)]
        pltpu.make_async_copy(block, block, x_recv.at[stage, far, zz]).wait()
        pltpu.make_async_remote_copy(
            block, block, m_send, m_recv.at[stage], device_id=(v, mate), device_id_type=MESH
        ).start()

    lane = lax.broadcasted_iota(jnp.int32, (BLOCKS, 128), 1)
    low = lane < EDGE
    fold = (
        lax.broadcasted_iota(jnp.int32, (EDGE, 128), 0) == (lane & (EDGE - 1))
    ).astype(F32).astype(BF)

    def arrive(stage):
        both = land.at[stage, pl.ds(0, 2)]
        pltpu.make_async_copy(both, both, m_recv.at[stage]).wait()
        for group in range(4):
            wide[group * size : (group + 1) * size, :] = land[stage, group].reshape(size, 128).astype(F32)

    def turn(stage, group, carry):
        pieces = []
        for row in range(STAGE_ROWS):
            piece = wide[pl.ds(group * size + row, BLOCKS, stride=STAGE_ROWS), :]
            pieces += [jnp.where(low, piece, 0.0).astype(BF), jnp.where(low, 0.0, piece).astype(BF)]
        turned = dot_t(fold, jnp.concatenate(pieces, axis=0))
        for row in range(STAGE_ROWS):
            tilt, step = (SPLIT, stage) if row == 15 else (STAGE_TILTS[stage][row // 3], row % 3)
            at = pl.multiple_of(group * (TILTS_HERE * BAND) + tilt * BAND + step * EDGE, EDGE)
            win[pl.ds(at, EDGE), :] = turned[:, row * 128 : (row + 1) * 128]
        return carry

    def parameters():
        heads = [wide[pl.ds(g * size + 2, 4, stride=3), :] for g in range(4)]
        heads = jnp.concatenate(heads + [jnp.zeros((112, 128), F32)], axis=0).T

        def spread(at):
            place = lax.broadcasted_iota(jnp.int32, (1, 128), 1)
            row = heads[at : at + 1]
            for j in range(1, 4):
                moved = pltpu.roll(jnp.broadcast_to(heads[at + 2 * j : at + 2 * j + 1], (8, 128)), 16 * j, 1)
                row = jnp.where((place >= 16 * j) & (place < 16 * j + 16), moved[0:1], row)
            return row

        tenths = spread(META) * 32.0 + spread(META + 1)
        base = spread(META + 64) * 64.0 + spread(META + 65)
        cosine, sine = trig_of(tenths)
        number = lax.broadcasted_iota(jnp.int32, (32, 128), 0)
        x_tile = ((number >> 3) * TILE + (v + core) * COLS).astype(F32)
        z_tile = ((number & 7) * TILE).astype(F32)
        coord = PIX / 2 + (x_tile - PIX / 2) * cosine + (z_tile - DEPTH / 2) * sine
        local = jnp.floor(coord + jnp.minimum((TILE - 1) * sine, 0.0)) - base
        local = jnp.clip(local.astype(jnp.int32), 0, BAND - 8 - WIN)
        place = lax.broadcasted_iota(jnp.int32, (32, 128), 1) & 63
        tilt_number = ((place >> 2) & 3) * TILTS_HERE + (place & 3) * 4 + (place >> 4)
        starts_v[...] = tilt_number * BAND + local
        to_smem = pltpu.make_async_copy(starts_v, starts_s, sem2)
        to_smem.start()
        offset = coord - (base + local.astype(F32))
        both = jnp.concatenate(
            [jnp.broadcast_to(cosine, (8, 128)), jnp.broadcast_to(sine, (8, 128))], axis=0
        )
        for g in range(STAGE_LANES[3] // 128):
            lanes = slice(g * 128, (g + 1) * 128)
            which = jnp.broadcast_to(lane_tilt[0:1, lanes], (32, 128))
            cst[:, lanes] = jnp.take_along_axis(offset, which, axis=1) - lane_pixel[0:1, lanes]
            trig[:, lanes] = jnp.take_along_axis(both, which[0:16], axis=1)
        to_smem.wait()

    def tile(stage, number, carry):
        chunks = STAGE_CHUNKS[stage]
        tilts = [(g, a) for g in range(4) for a in STAGE_TILTS[stage]]
        pad = sum(chunks) - WIN * len(tilts)
        right = [win[pl.ds(starts_s[number, 16 * (a % 4) + 4 * g + a // 4], WIN), :] for g, a in tilts]
        right = jnp.concatenate(right + [jnp.zeros((pad, 128), F32)], axis=0).astype(BF)
        here_rows = pl.ds(pl.multiple_of(number * 256, 256), 256)
        total = None if stage == 0 else acc[here_rows, :]
        at = 0
        origin = cst[pl.ds(number, 1), STAGE_LANES[stage] : STAGE_LANES[stage + 1]]
        for length in chunks:
            lanes = slice(STAGE_LANES[stage] + at, STAGE_LANES[stage] + at + length)
            cos_l = trig[0:1, lanes]
            zcol = lax.broadcasted_iota(jnp.int32, (TILE, length), 0).astype(F32)
            here = zcol * trig[8:9, lanes] + origin[:, at : at + length]
            pieces = []
            for _ in range(TILE):
                pieces.append(jnp.maximum(1.0 - jnp.abs(here.astype(BF)), jnp.zeros((), BF)))
                here = here + cos_l
            more = dot(jnp.concatenate(pieces, axis=0), right[at : at + length])
            total = more if total is None else total + more
            at += length
        if stage < 2:
            acc[here_rows, :] = total
            return carry
        rounded = total.astype(BF)
        xt, zt = number // 8, lax.rem(number, 8)
        for i in range(TILE):
            row = pl.multiple_of((xt * TILE + i) * DEPTH + zt * TILE, TILE)
            part[pl.ds(row, TILE), :] = rounded[i * TILE : (i + 1) * TILE]
        return carry

    filter_pairs(range(0, 3), *operands)
    pl.semaphore_wait(barrier, 65)
    send_stage(0)
    filter_pairs(range(3, 6), *operands)
    send_stage(1)
    filter_pairs(range(6, 8), *operands)
    send_stage(2)

    def loop_first(stage):
        def body(i, carry):
            pass_first(stage, i)
            return carry

        lax.fori_loop(0, 4, body, 0)

    def loop_second(stage):
        def body(i, carry):
            pass_second(stage, i)
            return carry

        lax.fori_loop(0, 4, body, 0)

    def spread_tiles(stage, low, high):
        lax.fori_loop(low, high, functools.partial(tile, stage), 0, unroll=2)

    loop_first(0)
    loop_second(0)
    loop_first(1)
    arrive(0)
    parameters()
    lax.fori_loop(0, 4, functools.partial(turn, 0), 0)
    spread_tiles(0, 0, 16)
    loop_second(1)
    loop_first(2)
    spread_tiles(0, 16, 32)
    arrive(1)
    lax.fori_loop(0, 4, functools.partial(turn, 1), 0)
    spread_tiles(1, 0, 16)
    loop_second(2)
    spread_tiles(1, 16, 32)
    arrive(2)
    lax.fori_loop(0, 4, functools.partial(turn, 2), 0)

    span = TILE * DEPTH
    copies = []
    for xt in range(4):
        spread_tiles(2, 8 * xt, 8 * xt + 8)
        slab = pl.ds(xt * span, span)
        there = pltpu.make_async_remote_copy(
            part.at[slab], other_ref.at[slab], send.at[xt], recv.at[xt],
            device_id=(v, mate), device_id_type=MESH,
        )
        here = pltpu.make_async_copy(part.at[slab], own_ref.at[slab], loc.at[xt])
        there.start()
        here.start()
        copies += [there, here]
    for copy in copies:
        copy.wait()
    sent = x_ref.at[:, pl.ds(0, 63)]
    pltpu.make_async_copy(sent, sent, a_send).wait()
    half = land.at[:, 0]
    pltpu.make_async_copy(half, half, x_send).wait()
    both = land.at[:, pl.ds(0, 2)]
    pltpu.make_async_copy(both, both, m_send).wait()


def box_kernel(own_ref, other_ref, corner_ref, owner_ref, box_out, vol_out, land, ext, lines, box_ref, vol_ref, sem, out_sem):
    v = lax.axis_index("vol")
    t = lax.axis_index("tilt")
    core = lax.rem(t, 2)
    half = CELLS // 2
    arrive = [
        pltpu.make_async_copy(own_ref, land.at[core], sem.at[0]),
        pltpu.make_async_copy(other_ref, land.at[1 - core], sem.at[1]),
    ]
    for copy in arrive:
        copy.start()
    picks = owner_ref.shape[1]
    owners = [owner_ref[0, r] for r in range(picks)]
    ranks = [sum([(owners[q] == owners[r]).astype(jnp.int32) for q in range(r)], jnp.int32(0)) for r in range(picks)]
    lane = lax.broadcasted_iota(jnp.int32, (BOX, 128), 1)
    y_of = (lane & 63) * 2 + (lane >> 6)
    line = lax.broadcasted_iota(jnp.int32, (BOX, 128), 0)
    quarter = (y_of == line + t * 32).astype(F32).astype(BF)[0:32]
    for copy in arrive:
        copy.wait()

    def slab(i, carry):
        rows = land[0, pl.ds(pl.multiple_of(i * 1024, 1024), 1024), :]
        both = dot_t(quarter, rows)
        for j in range(8):
            lines[pl.ds(i * 8 + j, 32, stride=COLS), :] = both[:, j * 128 : (j + 1) * 128]
        return carry

    lax.fori_loop(0, COLS // 8, slab, 0, unroll=2)
    for i in range(32):
        vol_ref[i] = lines[i * COLS : (i + 1) * COLS, :].astype(BF)
    copies = [pltpu.make_async_copy(vol_ref, vol_out, out_sem.at[4])]
    copies[0].start()
    for side in range(2):
        for i in range(8):
            ext[side * half + i * 1024 : side * half + (i + 1) * 1024, :] = land[
                side, i * 1024 : (i + 1) * 1024
            ].astype(F32)

    for slot in range(4):
        mine = [((owners[r] == t) & (ranks[r] == slot)).astype(jnp.int32) for r in range(picks)]
        present = sum(mine)
        x0 = sum([mine[r] * (corner_ref[0, r] - v * COLS) for r in range(picks)])
        y0 = sum([mine[r] * corner_ref[1, r] for r in range(picks)])
        z0 = sum([mine[r] * corner_ref[2, r] for r in range(picks)])
        chosen = ((y_of == line + y0) & (present > 0)).astype(F32).astype(BF)
        origin = x0 * DEPTH + z0

        def cut(i, carry):
            rows = jnp.concatenate(
                [ext[pl.ds(origin + (i * 8 + j) * DEPTH, BOX), :] for j in range(8)], axis=0
            ).astype(BF)
            box_ref[slot, :, pl.ds(pl.multiple_of(i * 512, 512), 512)] = dot_t(chosen, rows).astype(BF)
            return carry

        lax.fori_loop(0, BOX // 8, cut, 0, unroll=2)
        copies.append(pltpu.make_async_copy(box_ref.at[slot], box_out.at[slot], out_sem.at[slot]))
        copies[-1].start()
    for copy in copies:
        copy.wait()


def trig_of(tenths):
    angle = tenths.astype(F32) * (math.pi / 1800.0)
    return jnp.cos(angle), jnp.sin(angle)


def per_device(images, angle_tenths, dose_index, box_corner, box_owner):
    vm = pl.BlockSpec(memory_space=pltpu.VMEM)
    sm = pl.BlockSpec(memory_space=pltpu.SMEM)
    anym = pl.BlockSpec(memory_space=pl.ANY)
    dma = pltpu.SemaphoreType.DMA
    tables = [jnp.asarray(a) for a in fft_tables()]
    lane_tilt = np.zeros(STAGE_LANES[3], np.int32)
    lane_pixel = np.full(STAGE_LANES[3], -1.0e4, np.float32)
    for stage in range(3):
        tilts = [16 * (a % 4) + 4 * g + a // 4 for g in range(4) for a in STAGE_TILTS[stage]]
        at, count = STAGE_LANES[stage], WIN * len(tilts)
        lane_tilt[at : at + count] = np.repeat(np.array(tilts), WIN)
        lane_pixel[at : at + count] = np.tile(np.arange(WIN), len(tilts))
    lane_tilt = jnp.asarray(np.stack([lane_tilt] * 8))
    lane_pixel = jnp.asarray(np.stack([lane_pixel] * 8))
    part, other = pl.pallas_call(
        main_kernel,
        out_shape=(jax.ShapeDtypeStruct((CELLS // 2, 128), BF),) * 2,
        in_specs=[vm] * 6 + [sm] * 2 + [vm] * 2,
        out_specs=(anym, anym),
        scratch_shapes=[
            pltpu.VMEM((32 * 32, 128), F32),
            pltpu.VMEM((3 * BLOCKS * STAGE_ROWS, 128), F32),
            pltpu.VMEM((3, BLOCKS, STAGE_ROWS, 128), BF),
            pltpu.VMEM((3, 4, BLOCKS, STAGE_ROWS, 128), BF),
            pltpu.VMEM((4 * BLOCKS * STAGE_ROWS, 128), F32),
            pltpu.VMEM((TILTS * BAND, 128), F32),
            pltpu.VMEM((CELLS // 2, 128), F32),
            pltpu.VMEM((CELLS // 2, 128), BF),
            pltpu.VMEM((32, 128), jnp.int32),
            pltpu.SMEM((32, 128), jnp.int32),
            pltpu.VMEM((32, STAGE_LANES[3]), F32),
            pltpu.VMEM((16, STAGE_LANES[3]), F32),
            dma, dma((3, 2, 2)), dma, dma((3, 2, 2)), dma, dma((3,)),
            dma, dma((4,)), dma((4,)), dma((4,)),
        ],
        compiler_params=pltpu.CompilerParams(
            vmem_limit_bytes=VMEM_LIMIT, collective_id=1, has_side_effects=True
        ),
        name="main",
    )(images, *tables, angle_tenths.reshape(1, TILTS_HERE), angle_tenths, dose_index, lane_tilt, lane_pixel)

    boxes, volume = pl.pallas_call(
        box_kernel,
        out_shape=(
            jax.ShapeDtypeStruct((4, BOX, BOX * BOX), BF),
            jax.ShapeDtypeStruct((32, COLS, DEPTH), BF),
        ),
        in_specs=[anym, anym, sm, sm],
        out_specs=(anym, anym),
        scratch_shapes=[
            pltpu.VMEM((2, CELLS // 2, 128), BF),
            pltpu.VMEM((CELLS, 128), F32),
            pltpu.VMEM((32 * COLS, 128), F32),
            pltpu.VMEM((4, BOX, BOX * BOX), BF),
            pltpu.VMEM((32, COLS, DEPTH), BF),
            dma((2,)),
            dma((5,)),
        ],
        compiler_params=pltpu.CompilerParams(vmem_limit_bytes=VMEM_LIMIT),
        name="boxes",
    )(part, other, box_corner, box_owner.T)
    return volume, boxes.reshape(1, 1, 4, BOX, BOX * BOX)


def solution(mesh):
    in_specs = (P("tilt", "vol", None), P("tilt"), P("tilt"), P(None, "vol"), P("vol", None))
    out_specs = (P("tilt", "vol", None), P("vol", "tilt", None, None, None))
    return jax.shard_map(
        per_device, mesh=mesh, in_specs=in_specs, out_specs=out_specs, check_vma=False
    )
```

```python
import functools
import math

import jax
import jax.numpy as jnp
import ml_dtypes
import numpy as np
from jax import lax
from jax.experimental import pallas as pl
from jax.experimental.pallas import tpu as pltpu
from jax.sharding import PartitionSpec as P

MESH = pl.DeviceIdType.MESH
BF = jnp.bfloat16
F32 = jnp.float32

PIX = 4096
EDGE = 64
COLS = 64
DEPTH = 128
BOX = 64
BLOCKS = 64
TILTS_HERE = 16
TILTS = 64
BAND = 192
TILE = 16
WIN = 24
STAGE_ROWS = 16
SPLIT = 5
STAGE_TILTS = ((0, 1, 2, 3, 4), (6, 7, 8, 9, 10), (11, 12, 13, 14, 15, SPLIT))
STAGE_CHUNKS = ((256, 256), (256, 256), (256, 256, 128))
STAGE_LANES = (0, 512, 1024, 1792)
META = 56
CELLS = 2 * COLS * DEPTH

VMEM_LIMIT = 56 * 1024 * 1024


def split_np(table):
    high = table.astype(np.float32).astype(ml_dtypes.bfloat16)
    low = (table - high.astype(np.float64)).astype(np.float32).astype(ml_dtypes.bfloat16)
    return high, low


def fft_tables():
    grid = np.outer(np.arange(EDGE), np.arange(EDGE))
    cos_t = np.cos(2 * np.pi * (grid % EDGE) / EDGE)
    sin_t = np.sin(2 * np.pi * (grid % EDGE) / EDGE)
    stacked = np.concatenate([cos_t, sin_t], axis=0)
    s_hi, s_lo = split_np(stacked)
    left = np.concatenate([s_hi, s_lo], axis=0)
    order = np.concatenate([np.arange(0, EDGE, 2), np.arange(1, EDGE, 2)])
    left = np.stack([left[:, order], left])
    two = np.eye(2)
    cos2, sin2 = np.kron(two, cos_t), np.kron(two, sin_t)
    fwd = np.block([[cos2, -sin2], [sin2, cos2]])
    inv = np.block([[cos2, sin2], [-sin2, cos2]])
    f_hi, f_lo = split_np(fwd)
    i_hi, i_lo = split_np(inv)
    right = np.stack([f_hi, f_lo, i_hi, i_lo])
    twist = np.stack([np.cos(2 * np.pi * grid / PIX), np.sin(2 * np.pi * grid / PIX)])
    twist = np.concatenate([twist, twist], axis=2).astype(np.float32)
    k1, k2 = np.meshgrid(np.arange(EDGE), np.arange(EDGE), indexing="ij")
    freq = k1 + EDGE * k2
    freq = np.minimum(freq, PIX - freq)
    ratio = 2.0 * freq / PIX
    bend = ratio * np.sqrt(ratio)
    ramp = np.where(freq * 2 == PIX, 0.0, freq / PIX) / PIX
    shape = np.stack([bend, ramp])
    shape = np.concatenate([shape, shape], axis=2).astype(np.float32)
    return left, right, twist, shape


def dot(a, b):
    return jnp.dot(a, b, preferred_element_type=F32)


def dot_t(a, b):
    return lax.dot_general(a, b, (((1,), (1,)), ((), ())), preferred_element_type=F32)


def halves(value):
    high = value.astype(BF)
    return high, (value - high.astype(F32)).astype(BF)


def message_row(tilt, step):
    if tilt == SPLIT:
        return step, STAGE_ROWS - 1
    order = tilt - (tilt > SPLIT)
    return order // 5, 3 * (order % 5) + step


def filter_pairs(pairs, x_ref, left_ref, right_ref, twist_ref, shape_ref, angle_row, angle_ref, dose_ref, cube, scr):
    first_left, left = left_ref[0], left_ref[1]
    cos_w, sin_w = twist_ref[0], twist_ref[1]
    bend, ramp = shape_ref[0], shape_ref[1]
    lane = lax.broadcasted_iota(jnp.int32, (EDGE, 128), 1)
    first = lane < EDGE
    thin = first[0:32]
    n1 = lax.broadcasted_iota(jnp.int32, (BLOCKS, EDGE), 1)
    cosine, sine = trig_of(angle_row[...])
    columns = lax.broadcasted_iota(jnp.int32, (BLOCKS, TILTS_HERE), 0).astype(F32) * COLS
    lowest = (
        PIX / 2
        + (columns - PIX / 2) * cosine
        + jnp.minimum(-(DEPTH / 2) * sine, (DEPTH / 2 - 1) * sine)
    )
    begin = jnp.floor(lowest).astype(jnp.int32) - 1
    quots, rests = begin >> 6, begin & 63

    def side(row, pair):
        one = cube[pl.ds((pair * 4 + row) * 32, 32), :]
        two = cube[pl.ds((pair * 4 + 2 + row) * 32, 32), :]
        even = jnp.where(thin, one, pltpu.roll(two, EDGE, 1))
        odd = jnp.where(thin, pltpu.roll(one, EDGE, 1), two)
        return jnp.concatenate([even, odd], axis=0).astype(BF)

    for pair in pairs:
        part = dot(first_left, jnp.concatenate([side(0, pair), side(1, pair)], axis=1))
        cx = part[0:64] + part[128:192]
        sx = part[64:128] + part[192:256]
        re = cx[:, :128] + sx[:, 128:]
        im = cx[:, 128:] - sx[:, :128]
        turned = jnp.concatenate([re * cos_w + im * sin_w, im * cos_w - re * sin_w], axis=1)
        hi, lo = halves(turned)
        spec = dot(hi, right_ref[0]) + (dot(lo, right_ref[0]) + dot(hi, right_ref[1]))
        dose = jnp.where(first, dose_ref[2 * pair].astype(F32), dose_ref[2 * pair + 1].astype(F32))
        resp = ramp * jnp.exp((-0.05 * dose) * bend)
        spec = spec * jnp.concatenate([resp, resp], axis=1)
        hi, lo = halves(spec)
        back = dot(hi, right_ref[2]) + (dot(lo, right_ref[2]) + dot(hi, right_ref[3]))
        re, im = back[:, :128], back[:, 128:]
        turned = jnp.concatenate([re * cos_w - im * sin_w, im * cos_w + re * sin_w], axis=1)
        hi, lo = halves(turned)
        part = dot(left, hi)
        extra = dot(left[0:128], lo)
        cx = part[0:64] + (part[128:192] + extra[0:64])
        sx = part[64:128] + (part[192:256] + extra[64:128])
        re = cx[:, :128] - sx[:, 128:]
        im = cx[:, 128:] + sx[:, :128]
        rows = (
            jnp.where(first, re, pltpu.roll(im, EDGE, 1)),
            jnp.where(first, pltpu.roll(re, EDGE, 1), im),
        )
        for half in range(2):
            tilt = 2 * pair + half
            image = rows[half].astype(BF)
            quot = quots[:, tilt : tilt + 1]
            rest = rests[:, tilt : tilt + 1]
            pick = jnp.concatenate(
                [(n1 == quot + step).astype(F32).astype(BF) for step in range(4)], axis=0
            )
            near = dot(pick, image)
            at = (lane & EDGE) | ((lane + rest) & (EDGE - 1))
            stay = (lane & (EDGE - 1)) + rest < EDGE
            moved = [
                jnp.take_along_axis(near[step * EDGE : (step + 1) * EDGE], at, axis=1)
                for step in range(4)
            ]
            for step in range(3):
                piece = jnp.where(stay, moved[step], moved[step + 1])
                if step == 2 and tilt < 4:
                    for j in range(4):
                        other = 4 * tilt + j
                        tenths = angle_ref[other]
                        at_lane = META + 2 * j
                        piece = jnp.where(lane == at_lane, (tenths >> 5).astype(F32), piece)
                        piece = jnp.where(lane == at_lane + 1, (tenths & 31).astype(F32), piece)
                        quot_o = quots[:, other : other + 1].astype(F32)
                        rest_o = rests[:, other : other + 1].astype(F32)
                        piece = jnp.where(lane == at_lane + 64, quot_o, piece)
                        piece = jnp.where(lane == at_lane + 65, rest_o, piece)
                stage, row = message_row(tilt, step)
                scr[pl.ds(stage * BLOCKS * STAGE_ROWS + row, BLOCKS, stride=STAGE_ROWS), :] = piece


def main_kernel(
    image_ref, left_ref, right_ref, twist_ref, shape_ref, angle_row, angle_ref, dose_ref,
    lane_tilt, lane_pixel, own_ref, other_ref,
    cube, scr, x_ref, land, wide, win, acc, part, starts_v, starts_s, cst, trig,
    a_send, a_recv, x_send, x_recv, m_send, m_recv, sem2, loc, send, recv,
):
    v = lax.axis_index("vol")
    t = lax.axis_index("tilt")
    y, z, xh = lax.rem(v, 4), lax.rem(v // 4, 8), v // 32
    core, xl = lax.rem(t, 2), t // 2
    mate = xl * 2 + (1 - core)
    cross = (1 - xl) * 2 + core
    barrier = pltpu.get_barrier_semaphore()

    def greet(i, carry):
        p = lax.rem(xh * 32 + i, 64)
        q = jnp.where(i < 32, t, cross)

        @pl.when(p != v)
        def _():
            pl.semaphore_signal(barrier, inc=1, device_id=(p, q), device_id_type=MESH)

        return carry

    lax.fori_loop(0, 64, greet, 0)
    pl.semaphore_signal(barrier, inc=1, device_id=(v, cross), device_id_type=MESH)
    pl.semaphore_signal(barrier, inc=1, device_id=(v, mate), device_id_type=MESH)

    for tilt in range(TILTS_HERE):
        image = image_ref[tilt].astype(F32)
        for j in range(PIX // 128):
            cube[pl.ds(tilt * 64 + j, 2, stride=32), :] = image[:, j * 128 : (j + 1) * 128]

    operands = (image_ref, left_ref, right_ref, twist_ref, shape_ref, angle_row, angle_ref, dose_ref, cube, scr)
    steps = (0, 1, 7, 2, 6, 3, 5, 4)
    size = BLOCKS * STAGE_ROWS

    def send_stage(stage):
        x_ref[stage] = scr[stage * size : (stage + 1) * size, :].astype(BF).reshape(BLOCKS, STAGE_ROWS, 128)
        pltpu.make_async_copy(x_ref.at[stage, v], land.at[stage, t, v], a_recv.at[stage, 0, lax.div(z, 2)]).start()
        for dz in steps:
            for far in range(2):
                for dy in range(4):
                    if dz == 0 and far == 0 and dy == 0:
                        continue
                    zz, yy = lax.rem(z + dz, 8), lax.rem(y + dy, 4)
                    p = (xh if far == 0 else 1 - xh) * 32 + zz * 4 + yy
                    pltpu.make_async_remote_copy(
                        x_ref.at[stage, p],
                        land.at[stage, t, v],
                        a_send,
                        a_recv.at[stage, far, lax.div(z, 2)],
                        device_id=(p, t if far == 0 else cross),
                        device_id_type=MESH,
                    ).start()

    def chunk_of(i):
        far = lax.rem(i, 2)
        k = lax.div(i, 2)
        odd = lax.rem(k, 2)
        off = odd * lax.div(k + 1, 2) + (1 - odd) * lax.rem(4 - lax.div(k, 2), 4)
        planes = lax.rem(lax.div(z, 2) + off, 4)
        base = lax.rem(xh + far, 2) * 32 + planes * 8
        near_slot = lax.rem(xl + far, 2) * 2 + core
        far_slot = lax.rem(xl + far + 1, 2) * 2 + core
        return far, planes, base, near_slot, far_slot

    def pass_first(stage, i):
        far, zz, base, slot, _ = chunk_of(i)
        block = land.at[stage, slot, pl.ds(base, 8)]
        pltpu.make_async_copy(block, block, a_recv.at[stage, far, zz]).wait()
        pltpu.make_async_remote_copy(
            block, block, x_send, x_recv.at[stage, far, zz], device_id=(v, cross), device_id_type=MESH
        ).start()
        pltpu.make_async_remote_copy(
            block, block, m_send, m_recv.at[stage], device_id=(v, mate), device_id_type=MESH
        ).start()

    def pass_second(stage, i):
        far, zz, base, _, slot = chunk_of(i)
        block = land.at[stage, slot, pl.ds(base, 8)]
        pltpu.make_async_copy(block, block, x_recv.at[stage, far, zz]).wait()
        pltpu.make_async_remote_copy(
            block, block, m_send, m_recv.at[stage], device_id=(v, mate), device_id_type=MESH
        ).start()

    lane = lax.broadcasted_iota(jnp.int32, (BLOCKS, 128), 1)
    low = lane < EDGE
    fold = (
        lax.broadcasted_iota(jnp.int32, (EDGE, 128), 0) == (lane & (EDGE - 1))
    ).astype(F32).astype(BF)

    def arrive(stage):
        both = land.at[stage, pl.ds(0, 2)]
        pltpu.make_async_copy(both, both, m_recv.at[stage]).wait()
        for group in range(4):
            wide[group * size : (group + 1) * size, :] = land[stage, group].reshape(size, 128).astype(F32)

    def turn(stage, group, carry):
        pieces = []
        for row in range(STAGE_ROWS):
            piece = wide[pl.ds(group * size + row, BLOCKS, stride=STAGE_ROWS), :]
            pieces += [jnp.where(low, piece, 0.0).astype(BF), jnp.where(low, 0.0, piece).astype(BF)]
        turned = dot_t(fold, jnp.concatenate(pieces, axis=0))
        for row in range(STAGE_ROWS):
            tilt, step = (SPLIT, stage) if row == 15 else (STAGE_TILTS[stage][row // 3], row % 3)
            at = pl.multiple_of(group * (TILTS_HERE * BAND) + tilt * BAND + step * EDGE, EDGE)
            win[pl.ds(at, EDGE), :] = turned[:, row * 128 : (row + 1) * 128]
        return carry

    def parameters():
        heads = [wide[pl.ds(g * size + 2, 4, stride=3), :] for g in range(4)]
        heads = jnp.concatenate(heads + [jnp.zeros((112, 128), F32)], axis=0).T

        def spread(at):
            place = lax.broadcasted_iota(jnp.int32, (1, 128), 1)
            row = heads[at : at + 1]
            for j in range(1, 4):
                moved = pltpu.roll(jnp.broadcast_to(heads[at + 2 * j : at + 2 * j + 1], (8, 128)), 16 * j, 1)
                row = jnp.where((place >= 16 * j) & (place < 16 * j + 16), moved[0:1], row)
            return row

        tenths = spread(META) * 32.0 + spread(META + 1)
        base = spread(META + 64) * 64.0 + spread(META + 65)
        cosine, sine = trig_of(tenths)
        number = lax.broadcasted_iota(jnp.int32, (32, 128), 0)
        x_tile = ((number >> 3) * TILE + (v + core) * COLS).astype(F32)
        z_tile = ((number & 7) * TILE).astype(F32)
        coord = PIX / 2 + (x_tile - PIX / 2) * cosine + (z_tile - DEPTH / 2) * sine
        local = jnp.floor(coord + jnp.minimum((TILE - 1) * sine, 0.0)) - base
        local = jnp.clip(local.astype(jnp.int32), 0, BAND - 8 - WIN)
        place = lax.broadcasted_iota(jnp.int32, (32, 128), 1) & 63
        tilt_number = ((place >> 2) & 3) * TILTS_HERE + (place & 3) * 4 + (place >> 4)
        starts_v[...] = tilt_number * BAND + local
        to_smem = pltpu.make_async_copy(starts_v, starts_s, sem2)
        to_smem.start()
        offset = coord - (base + local.astype(F32))
        both = jnp.concatenate(
            [jnp.broadcast_to(cosine, (8, 128)), jnp.broadcast_to(sine, (8, 128))], axis=0
        )
        for g in range(STAGE_LANES[3] // 128):
            lanes = slice(g * 128, (g + 1) * 128)
            which = jnp.broadcast_to(lane_tilt[0:1, lanes], (32, 128))
            cst[:, lanes] = jnp.take_along_axis(offset, which, axis=1) - lane_pixel[0:1, lanes]
            trig[:, lanes] = jnp.take_along_axis(both, which[0:16], axis=1)
        to_smem.wait()

    def tile(stage, number, carry):
        chunks = STAGE_CHUNKS[stage]
        tilts = [(g, a) for g in range(4) for a in STAGE_TILTS[stage]]
        pad = sum(chunks) - WIN * len(tilts)
        right = [win[pl.ds(starts_s[number, 16 * (a % 4) + 4 * g + a // 4], WIN), :] for g, a in tilts]
        right = jnp.concatenate(right + [jnp.zeros((pad, 128), F32)], axis=0).astype(BF)
        here_rows = pl.ds(pl.multiple_of(number * 256, 256), 256)
        total = None if stage == 0 else acc[here_rows, :]
        at = 0
        origin = cst[pl.ds(number, 1), STAGE_LANES[stage] : STAGE_LANES[stage + 1]]
        for length in chunks:
            lanes = slice(STAGE_LANES[stage] + at, STAGE_LANES[stage] + at + length)
            cos_l = trig[0:1, lanes]
            zcol = lax.broadcasted_iota(jnp.int32, (TILE, length), 0).astype(F32)
            here = zcol * trig[8:9, lanes] + origin[:, at : at + length]
            pieces = []
            for _ in range(TILE):
                pieces.append(jnp.maximum(1.0 - jnp.abs(here.astype(BF)), jnp.zeros((), BF)))
                here = here + cos_l
            more = dot(jnp.concatenate(pieces, axis=0), right[at : at + length])
            total = more if total is None else total + more
            at += length
        if stage < 2:
            acc[here_rows, :] = total
            return carry
        rounded = total.astype(BF)
        xt, zt = number // 8, lax.rem(number, 8)
        for i in range(TILE):
            row = pl.multiple_of((xt * TILE + i) * DEPTH + zt * TILE, TILE)
            part[pl.ds(row, TILE), :] = rounded[i * TILE : (i + 1) * TILE]
        return carry

    def first(stage, low, high):
        def body(i, carry):
            pass_first(stage, i)
            return carry

        lax.fori_loop(low, high, body, 0)

    def second(stage):
        def body(i, carry):
            pass_second(stage, i)
            return carry

        lax.fori_loop(0, 8, body, 0)

    def turns(stage):
        lax.fori_loop(0, 4, functools.partial(turn, stage), 0, unroll=2)

    def tiles(stage, low, high):
        lax.fori_loop(low, high, functools.partial(tile, stage), 0, unroll=4)

    filter_pairs(range(0, 3), *operands)
    pl.semaphore_wait(barrier, 65)
    send_stage(0)
    filter_pairs(range(3, 6), *operands)
    send_stage(1)
    filter_pairs(range(6, 8), *operands)
    send_stage(2)
    first(0, 0, 8)
    second(0)
    first(1, 0, 8)
    arrive(0)
    parameters()
    turns(0)
    tiles(0, 0, 16)
    second(1)
    first(2, 0, 8)
    tiles(0, 16, 32)
    arrive(1)
    turns(1)
    tiles(1, 0, 16)
    second(2)
    tiles(1, 16, 32)
    arrive(2)
    turns(2)

    span = TILE * DEPTH
    copies = []
    for xt in range(4):
        tiles(2, 8 * xt, 8 * xt + 8)
        slab = pl.ds(xt * span, span)
        there = pltpu.make_async_remote_copy(
            part.at[slab], other_ref.at[slab], send.at[xt], recv.at[xt],
            device_id=(v, mate), device_id_type=MESH,
        )
        here = pltpu.make_async_copy(part.at[slab], own_ref.at[slab], loc.at[xt])
        there.start()
        here.start()
        copies += [there, here]
    for copy in copies:
        copy.wait()
    sent = x_ref.at[:, pl.ds(0, 63)]
    pltpu.make_async_copy(sent, sent, a_send).wait()
    half = land.at[:, 0]
    pltpu.make_async_copy(half, half, x_send).wait()
    both = land.at[:, pl.ds(0, 2)]
    pltpu.make_async_copy(both, both, m_send).wait()


def box_kernel(own_ref, other_ref, corner_ref, owner_ref, box_out, vol_out, land, ext, lines, box_ref, vol_ref, sem, out_sem):
    v = lax.axis_index("vol")
    t = lax.axis_index("tilt")
    core = lax.rem(t, 2)
    half = CELLS // 2
    arrive = [
        pltpu.make_async_copy(own_ref, land.at[core], sem.at[0]),
        pltpu.make_async_copy(other_ref, land.at[1 - core], sem.at[1]),
    ]
    for copy in arrive:
        copy.start()
    picks = owner_ref.shape[1]
    owners = [owner_ref[0, r] for r in range(picks)]
    ranks = [sum([(owners[q] == owners[r]).astype(jnp.int32) for q in range(r)], jnp.int32(0)) for r in range(picks)]
    lane = lax.broadcasted_iota(jnp.int32, (BOX, 128), 1)
    y_of = (lane & 63) * 2 + (lane >> 6)
    line = lax.broadcasted_iota(jnp.int32, (BOX, 128), 0)
    quarter = (y_of == line + t * 32).astype(F32).astype(BF)[0:32]
    for copy in arrive:
        copy.wait()

    def slab(i, carry):
        rows = land[0, pl.ds(pl.multiple_of(i * 1024, 1024), 1024), :]
        both = dot_t(quarter, rows)
        for j in range(8):
            lines[pl.ds(i * 8 + j, 32, stride=COLS), :] = both[:, j * 128 : (j + 1) * 128]
        return carry

    lax.fori_loop(0, COLS // 8, slab, 0, unroll=2)
    for i in range(32):
        vol_ref[i] = lines[i * COLS : (i + 1) * COLS, :].astype(BF)
    copies = [pltpu.make_async_copy(vol_ref, vol_out, out_sem.at[4])]
    copies[0].start()
    for side in range(2):
        for i in range(8):
            ext[side * half + i * 1024 : side * half + (i + 1) * 1024, :] = land[
                side, i * 1024 : (i + 1) * 1024
            ].astype(F32)

    for slot in range(4):
        mine = [((owners[r] == t) & (ranks[r] == slot)).astype(jnp.int32) for r in range(picks)]
        present = sum(mine)
        x0 = sum([mine[r] * (corner_ref[0, r] - v * COLS) for r in range(picks)])
        y0 = sum([mine[r] * corner_ref[1, r] for r in range(picks)])
        z0 = sum([mine[r] * corner_ref[2, r] for r in range(picks)])
        chosen = ((y_of == line + y0) & (present > 0)).astype(F32).astype(BF)
        origin = x0 * DEPTH + z0

        def cut(i, carry):
            rows = jnp.concatenate(
                [ext[pl.ds(origin + (i * 8 + j) * DEPTH, BOX), :] for j in range(8)], axis=0
            ).astype(BF)
            box_ref[slot, :, pl.ds(pl.multiple_of(i * 512, 512), 512)] = dot_t(chosen, rows).astype(BF)
            return carry

        lax.fori_loop(0, BOX // 8, cut, 0, unroll=8)
        copies.append(pltpu.make_async_copy(box_ref.at[slot], box_out.at[slot], out_sem.at[slot]))
        copies[-1].start()
    for copy in copies:
        copy.wait()


def trig_of(tenths):
    angle = tenths.astype(F32) * (math.pi / 1800.0)
    return jnp.cos(angle), jnp.sin(angle)


def per_device(images, angle_tenths, dose_index, box_corner, box_owner):
    vm = pl.BlockSpec(memory_space=pltpu.VMEM)
    sm = pl.BlockSpec(memory_space=pltpu.SMEM)
    anym = pl.BlockSpec(memory_space=pl.ANY)
    dma = pltpu.SemaphoreType.DMA
    tables = [jnp.asarray(a) for a in fft_tables()]
    lane_tilt = np.zeros(STAGE_LANES[3], np.int32)
    lane_pixel = np.full(STAGE_LANES[3], -1.0e4, np.float32)
    for stage in range(3):
        tilts = [16 * (a % 4) + 4 * g + a // 4 for g in range(4) for a in STAGE_TILTS[stage]]
        at, count = STAGE_LANES[stage], WIN * len(tilts)
        lane_tilt[at : at + count] = np.repeat(np.array(tilts), WIN)
        lane_pixel[at : at + count] = np.tile(np.arange(WIN), len(tilts))
    lane_tilt = jnp.asarray(np.stack([lane_tilt] * 8))
    lane_pixel = jnp.asarray(np.stack([lane_pixel] * 8))
    part, other = pl.pallas_call(
        main_kernel,
        out_shape=(jax.ShapeDtypeStruct((CELLS // 2, 128), BF),) * 2,
        in_specs=[vm] * 6 + [sm] * 2 + [vm] * 2,
        out_specs=(anym, anym),
        scratch_shapes=[
            pltpu.VMEM((32 * 32, 128), F32),
            pltpu.VMEM((3 * BLOCKS * STAGE_ROWS, 128), F32),
            pltpu.VMEM((3, BLOCKS, STAGE_ROWS, 128), BF),
            pltpu.VMEM((3, 4, BLOCKS, STAGE_ROWS, 128), BF),
            pltpu.VMEM((4 * BLOCKS * STAGE_ROWS, 128), F32),
            pltpu.VMEM((TILTS * BAND, 128), F32),
            pltpu.VMEM((CELLS // 2, 128), F32),
            pltpu.VMEM((CELLS // 2, 128), BF),
            pltpu.VMEM((32, 128), jnp.int32),
            pltpu.SMEM((32, 128), jnp.int32),
            pltpu.VMEM((32, STAGE_LANES[3]), F32),
            pltpu.VMEM((16, STAGE_LANES[3]), F32),
            dma, dma((3, 2, 4)), dma, dma((3, 2, 4)), dma, dma((3,)),
            dma, dma((4,)), dma((4,)), dma((4,)),
        ],
        compiler_params=pltpu.CompilerParams(
            vmem_limit_bytes=VMEM_LIMIT, collective_id=1, has_side_effects=True
        ),
        name="main",
    )(images, *tables, angle_tenths.reshape(1, TILTS_HERE), angle_tenths, dose_index, lane_tilt, lane_pixel)

    boxes, volume = pl.pallas_call(
        box_kernel,
        out_shape=(
            jax.ShapeDtypeStruct((4, BOX, BOX * BOX), BF),
            jax.ShapeDtypeStruct((32, COLS, DEPTH), BF),
        ),
        in_specs=[anym, anym, sm, sm],
        out_specs=(anym, anym),
        scratch_shapes=[
            pltpu.VMEM((2, CELLS // 2, 128), BF),
            pltpu.VMEM((CELLS, 128), F32),
            pltpu.VMEM((32 * COLS, 128), F32),
            pltpu.VMEM((4, BOX, BOX * BOX), BF),
            pltpu.VMEM((32, COLS, DEPTH), BF),
            dma((2,)),
            dma((5,)),
        ],
        compiler_params=pltpu.CompilerParams(vmem_limit_bytes=VMEM_LIMIT),
        name="boxes",
    )(part, other, box_corner, box_owner.T)
    return volume, boxes.reshape(1, 1, 4, BOX, BOX * BOX)


def solution(mesh):
    in_specs = (P("tilt", "vol", None), P("tilt"), P("tilt"), P(None, "vol"), P("vol", None))
    out_specs = (P("tilt", "vol", None), P("vol", "tilt", None, None, None))
    return jax.shard_map(
        per_device, mesh=mesh, in_specs=in_specs, out_specs=out_specs, check_vma=False
    )
```

```python
import functools
import math

import jax
import jax.numpy as jnp
import ml_dtypes
import numpy as np
from jax import lax
from jax.experimental import pallas as pl
from jax.experimental.pallas import tpu as pltpu
from jax.sharding import PartitionSpec as P

MESH = pl.DeviceIdType.MESH
BF = jnp.bfloat16
F32 = jnp.float32

PIX = 4096
EDGE = 64
COLS = 64
DEPTH = 128
BOX = 64
BLOCKS = 64
TILTS_HERE = 16
TILTS = 64
BAND = 192
TILE = 16
WIN = 24
STAGE_ROWS = 16
SPLIT = 5
STAGE_TILTS = ((0, 1, 2, 3, 4), (6, 7, 8, 9, 10), (11, 12, 13, 14, 15, SPLIT))
STAGE_CHUNKS = ((256, 256), (256, 256), (256, 256, 128))
STAGE_LANES = (0, 512, 1024, 1792)
META = 56
CELLS = 2 * COLS * DEPTH

VMEM_LIMIT = 56 * 1024 * 1024


def split_np(table):
    high = table.astype(np.float32).astype(ml_dtypes.bfloat16)
    low = (table - high.astype(np.float64)).astype(np.float32).astype(ml_dtypes.bfloat16)
    return high, low


def fft_tables():
    grid = np.outer(np.arange(EDGE), np.arange(EDGE))
    cos_t = np.cos(2 * np.pi * (grid % EDGE) / EDGE)
    sin_t = np.sin(2 * np.pi * (grid % EDGE) / EDGE)
    stacked = np.concatenate([cos_t, sin_t], axis=0)
    s_hi, s_lo = split_np(stacked)
    left = np.concatenate([s_hi, s_lo], axis=0)
    order = np.concatenate([np.arange(0, EDGE, 2), np.arange(1, EDGE, 2)])
    left = np.stack([left[:, order], left])
    two = np.eye(2)
    cos2, sin2 = np.kron(two, cos_t), np.kron(two, sin_t)
    fwd = np.block([[cos2, -sin2], [sin2, cos2]])
    inv = np.block([[cos2, sin2], [-sin2, cos2]])
    f_hi, f_lo = split_np(fwd)
    i_hi, i_lo = split_np(inv)
    right = np.stack([f_hi, f_lo, i_hi, i_lo])
    twist = np.stack([np.cos(2 * np.pi * grid / PIX), np.sin(2 * np.pi * grid / PIX)])
    twist = np.concatenate([twist, twist], axis=2).astype(np.float32)
    k1, k2 = np.meshgrid(np.arange(EDGE), np.arange(EDGE), indexing="ij")
    freq = k1 + EDGE * k2
    freq = np.minimum(freq, PIX - freq)
    ratio = 2.0 * freq / PIX
    bend = ratio * np.sqrt(ratio)
    ramp = np.where(freq * 2 == PIX, 0.0, freq / PIX) / PIX
    shape = np.stack([bend, ramp])
    shape = np.concatenate([shape, shape], axis=2).astype(np.float32)
    return left, right, twist, shape


def dot(a, b):
    return jnp.dot(a, b, preferred_element_type=F32)


def dot_t(a, b):
    return lax.dot_general(a, b, (((1,), (1,)), ((), ())), preferred_element_type=F32)


def halves(value):
    high = value.astype(BF)
    return high, (value - high.astype(F32)).astype(BF)


def message_row(tilt, step):
    if tilt == SPLIT:
        return step, STAGE_ROWS - 1
    order = tilt - (tilt > SPLIT)
    return order // 5, 3 * (order % 5) + step


def filter_pairs(pairs, x_ref, left_ref, right_ref, twist_ref, shape_ref, angle_row, angle_ref, dose_ref, cube, scr):
    first_left, left = left_ref[0], left_ref[1]
    cos_w, sin_w = twist_ref[0], twist_ref[1]
    bend, ramp = shape_ref[0], shape_ref[1]
    lane = lax.broadcasted_iota(jnp.int32, (EDGE, 128), 1)
    first = lane < EDGE
    thin = first[0:32]
    n1 = lax.broadcasted_iota(jnp.int32, (BLOCKS, EDGE), 1)
    cosine, sine = trig_of(angle_row[...])
    columns = lax.broadcasted_iota(jnp.int32, (BLOCKS, TILTS_HERE), 0).astype(F32) * COLS
    lowest = (
        PIX / 2
        + (columns - PIX / 2) * cosine
        + jnp.minimum(-(DEPTH / 2) * sine, (DEPTH / 2 - 1) * sine)
    )
    begin = jnp.floor(lowest).astype(jnp.int32) - 1
    quots, rests = begin >> 6, begin & 63

    def side(row, pair):
        one = cube[pl.ds((pair * 4 + row) * 32, 32), :]
        two = cube[pl.ds((pair * 4 + 2 + row) * 32, 32), :]
        even = jnp.where(thin, one, pltpu.roll(two, EDGE, 1))
        odd = jnp.where(thin, pltpu.roll(one, EDGE, 1), two)
        return jnp.concatenate([even, odd], axis=0).astype(BF)

    for pair in pairs:
        part = dot(first_left, jnp.concatenate([side(0, pair), side(1, pair)], axis=1))
        cx = part[0:64] + part[128:192]
        sx = part[64:128] + part[192:256]
        re = cx[:, :128] + sx[:, 128:]
        im = cx[:, 128:] - sx[:, :128]
        turned = jnp.concatenate([re * cos_w + im * sin_w, im * cos_w - re * sin_w], axis=1)
        hi, lo = halves(turned)
        spec = dot(hi, right_ref[0]) + (dot(lo, right_ref[0]) + dot(hi, right_ref[1]))
        dose = jnp.where(first, dose_ref[2 * pair].astype(F32), dose_ref[2 * pair + 1].astype(F32))
        resp = ramp * jnp.exp((-0.05 * dose) * bend)
        spec = spec * jnp.concatenate([resp, resp], axis=1)
        hi, lo = halves(spec)
        back = dot(hi, right_ref[2]) + (dot(lo, right_ref[2]) + dot(hi, right_ref[3]))
        re, im = back[:, :128], back[:, 128:]
        turned = jnp.concatenate([re * cos_w - im * sin_w, im * cos_w + re * sin_w], axis=1)
        hi, lo = halves(turned)
        part = dot(left, hi)
        extra = dot(left[0:128], lo)
        cx = part[0:64] + (part[128:192] + extra[0:64])
        sx = part[64:128] + (part[192:256] + extra[64:128])
        re = cx[:, :128] - sx[:, 128:]
        im = cx[:, 128:] + sx[:, :128]
        rows = (
            jnp.where(first, re, pltpu.roll(im, EDGE, 1)),
            jnp.where(first, pltpu.roll(re, EDGE, 1), im),
        )
        for half in range(2):
            tilt = 2 * pair + half
            image = rows[half].astype(BF)
            quot = quots[:, tilt : tilt + 1]
            rest = rests[:, tilt : tilt + 1]
            pick = jnp.concatenate(
                [(n1 == quot + step).astype(F32).astype(BF) for step in range(4)], axis=0
            )
            near = dot(pick, image)
            at = (lane & EDGE) | ((lane + rest) & (EDGE - 1))
            stay = (lane & (EDGE - 1)) + rest < EDGE
            moved = [
                jnp.take_along_axis(near[step * EDGE : (step + 1) * EDGE], at, axis=1)
                for step in range(4)
            ]
            for step in range(3):
                piece = jnp.where(stay, moved[step], moved[step + 1])
                if step == 2 and tilt < 4:
                    for j in range(4):
                        other = 4 * tilt + j
                        tenths = angle_ref[other]
                        at_lane = META + 2 * j
                        piece = jnp.where(lane == at_lane, (tenths >> 5).astype(F32), piece)
                        piece = jnp.where(lane == at_lane + 1, (tenths & 31).astype(F32), piece)
                        quot_o = quots[:, other : other + 1].astype(F32)
                        rest_o = rests[:, other : other + 1].astype(F32)
                        piece = jnp.where(lane == at_lane + 64, quot_o, piece)
                        piece = jnp.where(lane == at_lane + 65, rest_o, piece)
                stage, row = message_row(tilt, step)
                scr[pl.ds(stage * BLOCKS * STAGE_ROWS + row, BLOCKS, stride=STAGE_ROWS), :] = piece


def main_kernel(
    image_ref, left_ref, right_ref, twist_ref, shape_ref, angle_row, angle_ref, dose_ref,
    lane_tilt, lane_pixel, own_ref, other_ref,
    cube, scr, x_ref, land, wide, win, acc, part, starts_v, starts_s, cst, trig,
    a_send, a_recv, x_send, x_recv, m_send, m_recv, sem2, loc, send, recv,
):
    v = lax.axis_index("vol")
    t = lax.axis_index("tilt")
    y, z, xh = lax.rem(v, 4), lax.rem(v // 4, 8), v // 32
    core, xl = lax.rem(t, 2), t // 2
    mate = xl * 2 + (1 - core)
    cross = (1 - xl) * 2 + core
    barrier = pltpu.get_barrier_semaphore()

    def greet(i, carry):
        p = lax.rem(xh * 32 + i, 64)
        q = jnp.where(i < 32, t, cross)

        @pl.when(p != v)
        def _():
            pl.semaphore_signal(barrier, inc=1, device_id=(p, q), device_id_type=MESH)

        return carry

    lax.fori_loop(0, 64, greet, 0)
    pl.semaphore_signal(barrier, inc=1, device_id=(v, cross), device_id_type=MESH)
    pl.semaphore_signal(barrier, inc=1, device_id=(v, mate), device_id_type=MESH)

    for tilt in range(TILTS_HERE):
        image = image_ref[tilt].astype(F32)
        for j in range(PIX // 128):
            cube[pl.ds(tilt * 64 + j, 2, stride=32), :] = image[:, j * 128 : (j + 1) * 128]

    operands = (image_ref, left_ref, right_ref, twist_ref, shape_ref, angle_row, angle_ref, dose_ref, cube, scr)
    steps = (0, 1, 7, 2, 6, 3, 5, 4)
    size = BLOCKS * STAGE_ROWS

    def send_stage(stage):
        x_ref[stage] = scr[stage * size : (stage + 1) * size, :].astype(BF).reshape(BLOCKS, STAGE_ROWS, 128)
        pltpu.make_async_copy(x_ref.at[stage, v], land.at[stage, t, v], a_recv.at[stage, 0, lax.div(z, 2)]).start()
        for dz in steps:
            for far in range(2):
                for dy in range(4):
                    if dz == 0 and far == 0 and dy == 0:
                        continue
                    zz, yy = lax.rem(z + dz, 8), lax.rem(y + dy, 4)
                    p = (xh if far == 0 else 1 - xh) * 32 + zz * 4 + yy
                    pltpu.make_async_remote_copy(
                        x_ref.at[stage, p],
                        land.at[stage, t, v],
                        a_send,
                        a_recv.at[stage, far, lax.div(z, 2)],
                        device_id=(p, t if far == 0 else cross),
                        device_id_type=MESH,
                    ).start()

    def chunk_of(i):
        far = lax.rem(i, 2)
        k = lax.div(i, 2)
        odd = lax.rem(k, 2)
        off = odd * lax.div(k + 1, 2) + (1 - odd) * lax.rem(4 - lax.div(k, 2), 4)
        planes = lax.rem(lax.div(z, 2) + off, 4)
        base = lax.rem(xh + far, 2) * 32 + planes * 8
        near_slot = lax.rem(xl + far, 2) * 2 + core
        far_slot = lax.rem(xl + far + 1, 2) * 2 + core
        return far, planes, base, near_slot, far_slot

    def pass_first(stage, i):
        far, zz, base, slot, _ = chunk_of(i)
        block = land.at[stage, slot, pl.ds(base, 8)]
        pltpu.make_async_copy(block, block, a_recv.at[stage, far, zz]).wait()
        pltpu.make_async_remote_copy(
            block, block, x_send, x_recv.at[stage, far, zz], device_id=(v, cross), device_id_type=MESH
        ).start()
        pltpu.make_async_remote_copy(
            block, block, m_send, m_recv.at[stage], device_id=(v, mate), device_id_type=MESH
        ).start()

    def pass_second(stage, i):
        far, zz, base, _, slot = chunk_of(i)
        block = land.at[stage, slot, pl.ds(base, 8)]
        pltpu.make_async_copy(block, block, x_recv.at[stage, far, zz]).wait()
        pltpu.make_async_remote_copy(
            block, block, m_send, m_recv.at[stage], device_id=(v, mate), device_id_type=MESH
        ).start()

    lane = lax.broadcasted_iota(jnp.int32, (BLOCKS, 128), 1)
    low = lane < EDGE
    fold = (
        lax.broadcasted_iota(jnp.int32, (EDGE, 128), 0) == (lane & (EDGE - 1))
    ).astype(F32).astype(BF)

    def arrive(stage):
        both = land.at[stage, pl.ds(0, 2)]
        pltpu.make_async_copy(both, both, m_recv.at[stage]).wait()
        for group in range(4):
            wide[group * size : (group + 1) * size, :] = land[stage, group].reshape(size, 128).astype(F32)

    def turn(stage, group, carry):
        pieces = []
        for row in range(STAGE_ROWS):
            piece = wide[pl.ds(group * size + row, BLOCKS, stride=STAGE_ROWS), :]
            pieces += [jnp.where(low, piece, 0.0).astype(BF), jnp.where(low, 0.0, piece).astype(BF)]
        turned = dot_t(fold, jnp.concatenate(pieces, axis=0))
        for row in range(STAGE_ROWS):
            tilt, step = (SPLIT, stage) if row == 15 else (STAGE_TILTS[stage][row // 3], row % 3)
            at = pl.multiple_of(group * (TILTS_HERE * BAND) + tilt * BAND + step * EDGE, EDGE)
            win[pl.ds(at, EDGE), :] = turned[:, row * 128 : (row + 1) * 128]
        return carry

    def parameters():
        heads = [wide[pl.ds(g * size + 2, 4, stride=3), :] for g in range(4)]
        heads = jnp.concatenate(heads + [jnp.zeros((112, 128), F32)], axis=0).T

        def spread(at):
            place = lax.broadcasted_iota(jnp.int32, (1, 128), 1)
            row = heads[at : at + 1]
            for j in range(1, 4):
                moved = pltpu.roll(jnp.broadcast_to(heads[at + 2 * j : at + 2 * j + 1], (8, 128)), 16 * j, 1)
                row = jnp.where((place >= 16 * j) & (place < 16 * j + 16), moved[0:1], row)
            return row

        tenths = spread(META) * 32.0 + spread(META + 1)
        base = spread(META + 64) * 64.0 + spread(META + 65)
        cosine, sine = trig_of(tenths)
        number = lax.broadcasted_iota(jnp.int32, (32, 128), 0)
        x_tile = ((number >> 3) * TILE + (v + core) * COLS).astype(F32)
        z_tile = ((number & 7) * TILE).astype(F32)
        coord = PIX / 2 + (x_tile - PIX / 2) * cosine + (z_tile - DEPTH / 2) * sine
        local = jnp.floor(coord + jnp.minimum((TILE - 1) * sine, 0.0)) - base
        local = jnp.clip(local.astype(jnp.int32), 0, BAND - 8 - WIN)
        place = lax.broadcasted_iota(jnp.int32, (32, 128), 1) & 63
        tilt_number = ((place >> 2) & 3) * TILTS_HERE + (place & 3) * 4 + (place >> 4)
        starts_v[...] = tilt_number * BAND + local
        to_smem = pltpu.make_async_copy(starts_v, starts_s, sem2)
        to_smem.start()
        offset = coord - (base + local.astype(F32))
        both = jnp.concatenate(
            [jnp.broadcast_to(cosine, (8, 128)), jnp.broadcast_to(sine, (8, 128))], axis=0
        )
        for g in range(STAGE_LANES[3] // 128):
            lanes = slice(g * 128, (g + 1) * 128)
            which = jnp.broadcast_to(lane_tilt[0:1, lanes], (32, 128))
            cst[:, lanes] = jnp.take_along_axis(offset, which, axis=1) - lane_pixel[0:1, lanes]
            trig[:, lanes] = jnp.take_along_axis(both, which[0:16], axis=1)
        to_smem.wait()

    def tile(stage, number, carry):
        chunks = STAGE_CHUNKS[stage]
        tilts = [(g, a) for g in range(4) for a in STAGE_TILTS[stage]]
        pad = sum(chunks) - WIN * len(tilts)
        right = [win[pl.ds(starts_s[number, 16 * (a % 4) + 4 * g + a // 4], WIN), :] for g, a in tilts]
        right = jnp.concatenate(right + [jnp.zeros((pad, 128), F32)], axis=0).astype(BF)
        here_rows = pl.ds(pl.multiple_of(number * 256, 256), 256)
        total = None if stage == 0 else acc[here_rows, :]
        at = 0
        origin = cst[pl.ds(number, 1), STAGE_LANES[stage] : STAGE_LANES[stage + 1]]
        for length in chunks:
            lanes = slice(STAGE_LANES[stage] + at, STAGE_LANES[stage] + at + length)
            cos_l = trig[0:1, lanes]
            zcol = lax.broadcasted_iota(jnp.int32, (TILE, length), 0).astype(F32)
            here = zcol * trig[8:9, lanes] + origin[:, at : at + length]
            pieces = []
            for _ in range(TILE):
                pieces.append(jnp.maximum(1.0 - jnp.abs(here.astype(BF)), jnp.zeros((), BF)))
                here = here + cos_l
            more = dot(jnp.concatenate(pieces, axis=0), right[at : at + length])
            total = more if total is None else total + more
            at += length
        if stage < 2:
            acc[here_rows, :] = total
            return carry
        rounded = total.astype(BF)
        xt, zt = number // 8, lax.rem(number, 8)
        for i in range(TILE):
            part[xt * TILE + i, pl.ds(pl.multiple_of(zt * TILE, TILE), TILE), :] = rounded[i * TILE : (i + 1) * TILE]
        return carry

    def first(stage, low, high):
        def body(i, carry):
            pass_first(stage, i)
            return carry

        lax.fori_loop(low, high, body, 0)

    def second(stage):
        def body(i, carry):
            pass_second(stage, i)
            return carry

        lax.fori_loop(0, 8, body, 0)

    def turns(stage):
        lax.fori_loop(0, 4, functools.partial(turn, stage), 0, unroll=4)

    def tiles(stage, low, high):
        lax.fori_loop(low, high, functools.partial(tile, stage), 0, unroll=4)

    filter_pairs(range(0, 3), *operands)
    pl.semaphore_wait(barrier, 65)
    send_stage(0)
    filter_pairs(range(3, 6), *operands)
    send_stage(1)
    filter_pairs(range(6, 8), *operands)
    send_stage(2)
    first(0, 0, 8)
    second(0)
    first(1, 0, 8)
    arrive(0)
    parameters()
    turns(0)
    tiles(0, 0, 16)
    second(1)
    first(2, 0, 4)
    tiles(0, 16, 32)
    first(2, 4, 8)
    arrive(1)
    turns(1)
    tiles(1, 0, 24)
    second(2)
    tiles(1, 24, 32)
    arrive(2)
    turns(2)

    copies = []
    for k in range(8):
        tiles(2, 4 * k, 4 * k + 4)
        columns, depths = pl.ds((k // 2) * TILE, TILE), pl.ds((k % 2) * 64, 64)
        there = pltpu.make_async_remote_copy(
            part.at[columns, depths], other_ref.at[columns, depths], send.at[k], recv.at[k],
            device_id=(v, mate), device_id_type=MESH,
        )
        here = pltpu.make_async_copy(part.at[columns, depths], own_ref.at[columns, depths], loc.at[k])
        there.start()
        here.start()
        copies += [there, here]
    for copy in copies:
        copy.wait()
    sent = x_ref.at[:, pl.ds(0, 63)]
    pltpu.make_async_copy(sent, sent, a_send).wait()
    half = land.at[:, 0]
    pltpu.make_async_copy(half, half, x_send).wait()
    both = land.at[:, pl.ds(0, 2)]
    pltpu.make_async_copy(both, both, m_send).wait()


def box_kernel(own_ref, other_ref, corner_ref, owner_ref, box_out, vol_out, land, ext, lines, box_ref, vol_ref, sem, out_sem):
    v = lax.axis_index("vol")
    t = lax.axis_index("tilt")
    core = lax.rem(t, 2)
    half = CELLS // 2
    arrive = [
        pltpu.make_async_copy(own_ref, land.at[core], sem.at[core]),
        pltpu.make_async_copy(other_ref, land.at[1 - core], sem.at[1 - core]),
    ]
    for copy in arrive:
        copy.start()
    picks = owner_ref.shape[1]
    owners = [owner_ref[0, r] for r in range(picks)]
    ranks = [sum([(owners[q] == owners[r]).astype(jnp.int32) for q in range(r)], jnp.int32(0)) for r in range(picks)]
    lane = lax.broadcasted_iota(jnp.int32, (BOX, 128), 1)
    y_of = (lane & 63) * 2 + (lane >> 6)
    line = lax.broadcasted_iota(jnp.int32, (BOX, 128), 0)
    quarter = (y_of == line + t * 32).astype(F32).astype(BF)[0:32]
    pltpu.make_async_copy(own_ref, land.at[0], sem.at[0]).wait()

    def slab(i, carry):
        rows = land[0, pl.ds(pl.multiple_of(i * 1024, 1024), 1024), :]
        both = dot_t(quarter, rows)
        for j in range(8):
            lines[pl.ds(i * 8 + j, 32, stride=COLS), :] = both[:, j * 128 : (j + 1) * 128]
        return carry

    lax.fori_loop(0, COLS // 8, slab, 0, unroll=8)
    for i in range(32):
        vol_ref[i] = lines[i * COLS : (i + 1) * COLS, :].astype(BF)
    copies = [pltpu.make_async_copy(vol_ref, vol_out, out_sem.at[4])]
    copies[0].start()
    for side in range(2):
        if side == 1:
            pltpu.make_async_copy(own_ref, land.at[1], sem.at[1]).wait()
        for i in range(8):
            ext[side * half + i * 1024 : side * half + (i + 1) * 1024, :] = land[
                side, i * 1024 : (i + 1) * 1024
            ].astype(F32)

    for slot in range(4):
        mine = [((owners[r] == t) & (ranks[r] == slot)).astype(jnp.int32) for r in range(picks)]
        present = sum(mine)
        x0 = sum([mine[r] * (corner_ref[0, r] - v * COLS) for r in range(picks)])
        y0 = sum([mine[r] * corner_ref[1, r] for r in range(picks)])
        z0 = sum([mine[r] * corner_ref[2, r] for r in range(picks)])
        chosen = ((y_of == line + y0) & (present > 0)).astype(F32).astype(BF)
        origin = x0 * DEPTH + z0

        def cut(i, carry):
            rows = jnp.concatenate(
                [ext[pl.ds(origin + (i * 8 + j) * DEPTH, BOX), :] for j in range(8)], axis=0
            ).astype(BF)
            box_ref[slot, :, pl.ds(pl.multiple_of(i * 512, 512), 512)] = dot_t(chosen, rows).astype(BF)
            return carry

        lax.fori_loop(0, BOX // 8, cut, 0, unroll=8)
        copies.append(pltpu.make_async_copy(box_ref.at[slot], box_out.at[slot], out_sem.at[slot]))
        copies[-1].start()
    for copy in copies:
        copy.wait()


def trig_of(tenths):
    angle = tenths.astype(F32) * (math.pi / 1800.0)
    return jnp.cos(angle), jnp.sin(angle)


def per_device(images, angle_tenths, dose_index, box_corner, box_owner):
    vm = pl.BlockSpec(memory_space=pltpu.VMEM)
    sm = pl.BlockSpec(memory_space=pltpu.SMEM)
    anym = pl.BlockSpec(memory_space=pl.ANY)
    dma = pltpu.SemaphoreType.DMA
    tables = [jnp.asarray(a) for a in fft_tables()]
    lane_tilt = np.zeros(STAGE_LANES[3], np.int32)
    lane_pixel = np.full(STAGE_LANES[3], -1.0e4, np.float32)
    for stage in range(3):
        tilts = [16 * (a % 4) + 4 * g + a // 4 for g in range(4) for a in STAGE_TILTS[stage]]
        at, count = STAGE_LANES[stage], WIN * len(tilts)
        lane_tilt[at : at + count] = np.repeat(np.array(tilts), WIN)
        lane_pixel[at : at + count] = np.tile(np.arange(WIN), len(tilts))
    lane_tilt = jnp.asarray(np.stack([lane_tilt] * 8))
    lane_pixel = jnp.asarray(np.stack([lane_pixel] * 8))
    part, other = pl.pallas_call(
        main_kernel,
        out_shape=(jax.ShapeDtypeStruct((COLS, DEPTH, 128), BF),) * 2,
        in_specs=[vm] * 6 + [sm] * 2 + [vm] * 2,
        out_specs=(anym, anym),
        scratch_shapes=[
            pltpu.VMEM((32 * 32, 128), F32),
            pltpu.VMEM((3 * BLOCKS * STAGE_ROWS, 128), F32),
            pltpu.VMEM((3, BLOCKS, STAGE_ROWS, 128), BF),
            pltpu.VMEM((3, 4, BLOCKS, STAGE_ROWS, 128), BF),
            pltpu.VMEM((4 * BLOCKS * STAGE_ROWS, 128), F32),
            pltpu.VMEM((TILTS * BAND, 128), F32),
            pltpu.VMEM((CELLS // 2, 128), F32),
            pltpu.VMEM((COLS, DEPTH, 128), BF),
            pltpu.VMEM((32, 128), jnp.int32),
            pltpu.SMEM((32, 128), jnp.int32),
            pltpu.VMEM((32, STAGE_LANES[3]), F32),
            pltpu.VMEM((16, STAGE_LANES[3]), F32),
            dma, dma((3, 2, 4)), dma, dma((3, 2, 4)), dma, dma((3,)),
            dma, dma((8,)), dma((8,)), dma((8,)),
        ],
        compiler_params=pltpu.CompilerParams(
            vmem_limit_bytes=VMEM_LIMIT, collective_id=1, has_side_effects=True
        ),
        name="main",
    )(images, *tables, angle_tenths.reshape(1, TILTS_HERE), angle_tenths, dose_index, lane_tilt, lane_pixel)

    boxes, volume = pl.pallas_call(
        box_kernel,
        out_shape=(
            jax.ShapeDtypeStruct((4, BOX, BOX * BOX), BF),
            jax.ShapeDtypeStruct((32, COLS, DEPTH), BF),
        ),
        in_specs=[anym, anym, sm, sm],
        out_specs=(anym, anym),
        scratch_shapes=[
            pltpu.VMEM((2, CELLS // 2, 128), BF),
            pltpu.VMEM((CELLS, 128), F32),
            pltpu.VMEM((32 * COLS, 128), F32),
            pltpu.VMEM((4, BOX, BOX * BOX), BF),
            pltpu.VMEM((32, COLS, DEPTH), BF),
            dma((2,)),
            dma((5,)),
        ],
        compiler_params=pltpu.CompilerParams(vmem_limit_bytes=VMEM_LIMIT),
        name="boxes",
    )(part.reshape(CELLS // 2, 128), other.reshape(CELLS // 2, 128), box_corner, box_owner.T)
    return volume, boxes.reshape(1, 1, 4, BOX, BOX * BOX)


def solution(mesh):
    in_specs = (P("tilt", "vol", None), P("tilt"), P("tilt"), P(None, "vol"), P("vol", None))
    out_specs = (P("tilt", "vol", None), P("vol", "tilt", None, None, None))
    return jax.shard_map(
        per_device, mesh=mesh, in_specs=in_specs, out_specs=out_specs, check_vma=False
    )
```

```python
import functools
import math

import jax
import jax.numpy as jnp
import ml_dtypes
import numpy as np
from jax import lax
from jax.experimental import pallas as pl
from jax.experimental.pallas import tpu as pltpu
from jax.sharding import PartitionSpec as P

MESH = pl.DeviceIdType.MESH
BF = jnp.bfloat16
F32 = jnp.float32

PIX = 4096
EDGE = 64
COLS = 64
DEPTH = 128
BOX = 64
BLOCKS = 64
TILTS_HERE = 16
TILTS = 64
BAND = 192
TILE = 16
WIN = 24
STAGE_ROWS = 16
SPLIT = 5
STAGE_TILTS = ((0, 1, 2, 3, 4), (6, 7, 8, 9, 10), (11, 12, 13, 14, 15, SPLIT))
STAGE_CHUNKS = ((256, 256), (256, 256), (256, 256, 128))
STAGE_LANES = (0, 512, 1024, 1792)
META = 56
CELLS = 2 * COLS * DEPTH

VMEM_LIMIT = 56 * 1024 * 1024


def split_np(table):
    high = table.astype(np.float32).astype(ml_dtypes.bfloat16)
    low = (table - high.astype(np.float64)).astype(np.float32).astype(ml_dtypes.bfloat16)
    return high, low


def fft_tables():
    grid = np.outer(np.arange(EDGE), np.arange(EDGE))
    cos_t = np.cos(2 * np.pi * (grid % EDGE) / EDGE)
    sin_t = np.sin(2 * np.pi * (grid % EDGE) / EDGE)
    stacked = np.concatenate([cos_t, sin_t], axis=0)
    s_hi, s_lo = split_np(stacked)
    left = np.concatenate([s_hi, s_lo], axis=0)
    order = np.concatenate([np.arange(0, EDGE, 2), np.arange(1, EDGE, 2)])
    left = np.stack([left[:, order], left])
    two = np.eye(2)
    cos2, sin2 = np.kron(two, cos_t), np.kron(two, sin_t)
    fwd = np.block([[cos2, -sin2], [sin2, cos2]])
    inv = np.block([[cos2, sin2], [-sin2, cos2]])
    f_hi, f_lo = split_np(fwd)
    i_hi, i_lo = split_np(inv)
    right = np.stack([f_hi, f_lo, i_hi, i_lo])
    twist = np.stack([np.cos(2 * np.pi * grid / PIX), np.sin(2 * np.pi * grid / PIX)])
    twist = np.concatenate([twist, twist], axis=2).astype(np.float32)
    k1, k2 = np.meshgrid(np.arange(EDGE), np.arange(EDGE), indexing="ij")
    freq = k1 + EDGE * k2
    freq = np.minimum(freq, PIX - freq)
    ratio = 2.0 * freq / PIX
    bend = ratio * np.sqrt(ratio)
    ramp = np.where(freq * 2 == PIX, 0.0, freq / PIX) / PIX
    shape = np.stack([bend, ramp])
    shape = np.concatenate([shape, shape], axis=2).astype(np.float32)
    return left, right, twist, shape


def dot(a, b):
    return jnp.dot(a, b, preferred_element_type=F32)


def dot_t(a, b):
    return lax.dot_general(a, b, (((1,), (1,)), ((), ())), preferred_element_type=F32)


def halves(value):
    high = value.astype(BF)
    return high, (value - high.astype(F32)).astype(BF)


def message_row(tilt, step):
    if tilt == SPLIT:
        return step, STAGE_ROWS - 1
    order = tilt - (tilt > SPLIT)
    return order // 5, 3 * (order % 5) + step


def filter_pairs(pairs, x_ref, left_ref, right_ref, twist_ref, shape_ref, angle_row, angle_ref, dose_ref, cube, scr):
    first_left, left = left_ref[0], left_ref[1]
    cos_w, sin_w = twist_ref[0], twist_ref[1]
    bend, ramp = shape_ref[0], shape_ref[1]
    lane = lax.broadcasted_iota(jnp.int32, (EDGE, 128), 1)
    first = lane < EDGE
    thin = first[0:32]
    n1 = lax.broadcasted_iota(jnp.int32, (BLOCKS, EDGE), 1)
    cosine, sine = trig_of(angle_row[...])
    columns = lax.broadcasted_iota(jnp.int32, (BLOCKS, TILTS_HERE), 0).astype(F32) * COLS
    lowest = (
        PIX / 2
        + (columns - PIX / 2) * cosine
        + jnp.minimum(-(DEPTH / 2) * sine, (DEPTH / 2 - 1) * sine)
    )
    begin = jnp.floor(lowest).astype(jnp.int32) - 1
    quots, rests = begin >> 6, begin & 63

    def side(row, pair):
        one = cube[pl.ds((pair * 4 + row) * 32, 32), :]
        two = cube[pl.ds((pair * 4 + 2 + row) * 32, 32), :]
        even = jnp.where(thin, one, pltpu.roll(two, EDGE, 1))
        odd = jnp.where(thin, pltpu.roll(one, EDGE, 1), two)
        return jnp.concatenate([even, odd], axis=0).astype(BF)

    for pair in pairs:
        part = dot(first_left, jnp.concatenate([side(0, pair), side(1, pair)], axis=1))
        cx = part[0:64] + part[128:192]
        sx = part[64:128] + part[192:256]
        re = cx[:, :128] + sx[:, 128:]
        im = cx[:, 128:] - sx[:, :128]
        turned = jnp.concatenate([re * cos_w + im * sin_w, im * cos_w - re * sin_w], axis=1)
        hi, lo = halves(turned)
        spec = dot(hi, right_ref[0]) + (dot(lo, right_ref[0]) + dot(hi, right_ref[1]))
        dose = jnp.where(first, dose_ref[2 * pair].astype(F32), dose_ref[2 * pair + 1].astype(F32))
        resp = ramp * jnp.exp((-0.05 * dose) * bend)
        spec = spec * jnp.concatenate([resp, resp], axis=1)
        hi, lo = halves(spec)
        back = dot(hi, right_ref[2]) + (dot(lo, right_ref[2]) + dot(hi, right_ref[3]))
        re, im = back[:, :128], back[:, 128:]
        turned = jnp.concatenate([re * cos_w - im * sin_w, im * cos_w + re * sin_w], axis=1)
        hi, lo = halves(turned)
        part = dot(left, hi)
        extra = dot(left[0:128], lo)
        cx = part[0:64] + (part[128:192] + extra[0:64])
        sx = part[64:128] + (part[192:256] + extra[64:128])
        re = cx[:, :128] - sx[:, 128:]
        im = cx[:, 128:] + sx[:, :128]
        rows = (
            jnp.where(first, re, pltpu.roll(im, EDGE, 1)),
            jnp.where(first, pltpu.roll(re, EDGE, 1), im),
        )
        for half in range(2):
            tilt = 2 * pair + half
            image = rows[half].astype(BF)
            quot = quots[:, tilt : tilt + 1]
            rest = rests[:, tilt : tilt + 1]
            pick = jnp.concatenate(
                [(n1 == quot + step).astype(F32).astype(BF) for step in range(4)], axis=0
            )
            near = dot(pick, image)
            at = (lane & EDGE) | ((lane + rest) & (EDGE - 1))
            stay = (lane & (EDGE - 1)) + rest < EDGE
            moved = [
                jnp.take_along_axis(near[step * EDGE : (step + 1) * EDGE], at, axis=1)
                for step in range(4)
            ]
            for step in range(3):
                piece = jnp.where(stay, moved[step], moved[step + 1])
                if step == 2 and tilt < 4:
                    for j in range(4):
                        other = 4 * tilt + j
                        tenths = angle_ref[other]
                        at_lane = META + 2 * j
                        piece = jnp.where(lane == at_lane, (tenths >> 5).astype(F32), piece)
                        piece = jnp.where(lane == at_lane + 1, (tenths & 31).astype(F32), piece)
                        quot_o = quots[:, other : other + 1].astype(F32)
                        rest_o = rests[:, other : other + 1].astype(F32)
                        piece = jnp.where(lane == at_lane + 64, quot_o, piece)
                        piece = jnp.where(lane == at_lane + 65, rest_o, piece)
                stage, row = message_row(tilt, step)
                scr[pl.ds(stage * BLOCKS * STAGE_ROWS + row, BLOCKS, stride=STAGE_ROWS), :] = piece


def main_kernel(
    image_ref, left_ref, right_ref, twist_ref, shape_ref, angle_row, angle_ref, dose_ref,
    lane_tilt, lane_pixel, own_ref, other_ref,
    cube, scr, x_ref, land, wide, win, acc, part, starts_v, starts_s, cst, trig,
    a_send, a_recv, x_send, x_recv, m_send, m_recv, sem2, loc, send, recv,
):
    v = lax.axis_index("vol")
    t = lax.axis_index("tilt")
    y, z, xh = lax.rem(v, 4), lax.rem(v // 4, 8), v // 32
    core, xl = lax.rem(t, 2), t // 2
    mate = xl * 2 + (1 - core)
    cross = (1 - xl) * 2 + core
    barrier = pltpu.get_barrier_semaphore()

    def greet(i, carry):
        p = lax.rem(xh * 32 + i, 64)
        q = jnp.where(i < 32, t, cross)

        @pl.when(p != v)
        def _():
            pl.semaphore_signal(barrier, inc=1, device_id=(p, q), device_id_type=MESH)

        return carry

    lax.fori_loop(0, 64, greet, 0)
    pl.semaphore_signal(barrier, inc=1, device_id=(v, cross), device_id_type=MESH)
    pl.semaphore_signal(barrier, inc=1, device_id=(v, mate), device_id_type=MESH)

    for tilt in range(TILTS_HERE):
        image = image_ref[tilt].astype(F32)
        for j in range(PIX // 128):
            cube[pl.ds(tilt * 64 + j, 2, stride=32), :] = image[:, j * 128 : (j + 1) * 128]

    operands = (image_ref, left_ref, right_ref, twist_ref, shape_ref, angle_row, angle_ref, dose_ref, cube, scr)
    steps = (0, 1, 7, 2, 6, 3, 5, 4)
    size = BLOCKS * STAGE_ROWS

    def send_stage(stage):
        x_ref[stage] = scr[stage * size : (stage + 1) * size, :].astype(BF).reshape(BLOCKS, STAGE_ROWS, 128)
        pltpu.make_async_copy(x_ref.at[stage, v], land.at[stage, t, v], a_recv.at[stage, 0, lax.div(z, 2)]).start()
        for dz in steps:
            for far in range(2):
                for dy in range(4):
                    if dz == 0 and far == 0 and dy == 0:
                        continue
                    zz, yy = lax.rem(z + dz, 8), lax.rem(y + dy, 4)
                    p = (xh if far == 0 else 1 - xh) * 32 + zz * 4 + yy
                    pltpu.make_async_remote_copy(
                        x_ref.at[stage, p],
                        land.at[stage, t, v],
                        a_send,
                        a_recv.at[stage, far, lax.div(z, 2)],
                        device_id=(p, t if far == 0 else cross),
                        device_id_type=MESH,
                    ).start()

    def chunk_of(i):
        far = lax.rem(i, 2)
        k = lax.div(i, 2)
        odd = lax.rem(k, 2)
        off = odd * lax.div(k + 1, 2) + (1 - odd) * lax.rem(4 - lax.div(k, 2), 4)
        planes = lax.rem(lax.div(z, 2) + off, 4)
        base = lax.rem(xh + far, 2) * 32 + planes * 8
        near_slot = lax.rem(xl + far, 2) * 2 + core
        far_slot = lax.rem(xl + far + 1, 2) * 2 + core
        return far, planes, base, near_slot, far_slot

    def pass_first(stage, i):
        far, zz, base, slot, _ = chunk_of(i)
        block = land.at[stage, slot, pl.ds(base, 8)]
        pltpu.make_async_copy(block, block, a_recv.at[stage, far, zz]).wait()
        pltpu.make_async_remote_copy(
            block, block, x_send, x_recv.at[stage, far, zz], device_id=(v, cross), device_id_type=MESH
        ).start()
        pltpu.make_async_remote_copy(
            block, block, m_send, m_recv.at[stage], device_id=(v, mate), device_id_type=MESH
        ).start()

    def pass_second(stage, i):
        far, zz, base, _, slot = chunk_of(i)
        block = land.at[stage, slot, pl.ds(base, 8)]
        pltpu.make_async_copy(block, block, x_recv.at[stage, far, zz]).wait()
        pltpu.make_async_remote_copy(
            block, block, m_send, m_recv.at[stage], device_id=(v, mate), device_id_type=MESH
        ).start()

    lane = lax.broadcasted_iota(jnp.int32, (BLOCKS, 128), 1)
    low = lane < EDGE
    fold = (
        lax.broadcasted_iota(jnp.int32, (EDGE, 128), 0) == (lane & (EDGE - 1))
    ).astype(F32).astype(BF)

    def arrive(stage):
        both = land.at[stage, pl.ds(0, 2)]
        pltpu.make_async_copy(both, both, m_recv.at[stage]).wait()
        for group in range(4):
            wide[group * size : (group + 1) * size, :] = land[stage, group].reshape(size, 128).astype(F32)

    def turn(stage, group, carry):
        pieces = []
        for row in range(STAGE_ROWS):
            piece = wide[pl.ds(group * size + row, BLOCKS, stride=STAGE_ROWS), :]
            pieces += [jnp.where(low, piece, 0.0).astype(BF), jnp.where(low, 0.0, piece).astype(BF)]
        turned = dot_t(fold, jnp.concatenate(pieces, axis=0))
        for row in range(STAGE_ROWS):
            tilt, step = (SPLIT, stage) if row == 15 else (STAGE_TILTS[stage][row // 3], row % 3)
            at = pl.multiple_of(group * (TILTS_HERE * BAND) + tilt * BAND + step * EDGE, EDGE)
            win[pl.ds(at, EDGE), :] = turned[:, row * 128 : (row + 1) * 128]
        return carry

    def parameters():
        heads = [wide[pl.ds(g * size + 2, 4, stride=3), :] for g in range(4)]
        heads = jnp.concatenate(heads + [jnp.zeros((112, 128), F32)], axis=0).T

        def spread(at):
            place = lax.broadcasted_iota(jnp.int32, (1, 128), 1)
            row = heads[at : at + 1]
            for j in range(1, 4):
                moved = pltpu.roll(jnp.broadcast_to(heads[at + 2 * j : at + 2 * j + 1], (8, 128)), 16 * j, 1)
                row = jnp.where((place >= 16 * j) & (place < 16 * j + 16), moved[0:1], row)
            return row

        tenths = spread(META) * 32.0 + spread(META + 1)
        base = spread(META + 64) * 64.0 + spread(META + 65)
        cosine, sine = trig_of(tenths)
        number = lax.broadcasted_iota(jnp.int32, (32, 128), 0)
        x_tile = ((number >> 3) * TILE + (v + core) * COLS).astype(F32)
        z_tile = ((number & 7) * TILE).astype(F32)
        coord = PIX / 2 + (x_tile - PIX / 2) * cosine + (z_tile - DEPTH / 2) * sine
        local = jnp.floor(coord + jnp.minimum((TILE - 1) * sine, 0.0)) - base
        local = jnp.clip(local.astype(jnp.int32), 0, BAND - 8 - WIN)
        place = lax.broadcasted_iota(jnp.int32, (32, 128), 1) & 63
        tilt_number = ((place >> 2) & 3) * TILTS_HERE + (place & 3) * 4 + (place >> 4)
        starts_v[...] = tilt_number * BAND + local
        to_smem = pltpu.make_async_copy(starts_v, starts_s, sem2)
        to_smem.start()
        offset = coord - (base + local.astype(F32))
        both = jnp.concatenate(
            [jnp.broadcast_to(cosine, (8, 128)), jnp.broadcast_to(sine, (8, 128))], axis=0
        )
        for g in range(STAGE_LANES[3] // 128):
            lanes = slice(g * 128, (g + 1) * 128)
            which = jnp.broadcast_to(lane_tilt[0:1, lanes], (32, 128))
            cst[:, lanes] = jnp.take_along_axis(offset, which, axis=1) - lane_pixel[0:1, lanes]
            trig[:, lanes] = jnp.take_along_axis(both, which[0:16], axis=1)
        to_smem.wait()

    def tile(stage, number, carry):
        chunks = STAGE_CHUNKS[stage]
        tilts = [(g, a) for g in range(4) for a in STAGE_TILTS[stage]]
        pad = sum(chunks) - WIN * len(tilts)
        right = [win[pl.ds(starts_s[number, 16 * (a % 4) + 4 * g + a // 4], WIN), :] for g, a in tilts]
        right = jnp.concatenate(right + [jnp.zeros((pad, 128), F32)], axis=0).astype(BF)
        here_rows = pl.ds(pl.multiple_of(number * 256, 256), 256)
        total = None if stage == 0 else acc[here_rows, :]
        at = 0
        origin = cst[pl.ds(number, 1), STAGE_LANES[stage] : STAGE_LANES[stage + 1]]
        for length in chunks:
            lanes = slice(STAGE_LANES[stage] + at, STAGE_LANES[stage] + at + length)
            cos_l = trig[0:1, lanes]
            zcol = lax.broadcasted_iota(jnp.int32, (TILE, length), 0).astype(F32)
            here = zcol * trig[8:9, lanes] + origin[:, at : at + length]
            pieces = []
            for _ in range(TILE):
                pieces.append(jnp.maximum(1.0 - jnp.abs(here.astype(BF)), jnp.zeros((), BF)))
                here = here + cos_l
            more = dot(jnp.concatenate(pieces, axis=0), right[at : at + length])
            total = more if total is None else total + more
            at += length
        if stage < 2:
            acc[here_rows, :] = total
            return carry
        rounded = total.astype(BF)
        xt, zt = number // 8, lax.rem(number, 8)
        for i in range(TILE):
            part[xt * TILE + i, pl.ds(pl.multiple_of(zt * TILE, TILE), TILE), :] = rounded[i * TILE : (i + 1) * TILE]
        return carry

    def first(stage, low, high):
        def body(i, carry):
            pass_first(stage, i)
            return carry

        lax.fori_loop(low, high, body, 0)

    def second(stage):
        def body(i, carry):
            pass_second(stage, i)
            return carry

        lax.fori_loop(0, 8, body, 0)

    def turns(stage):
        lax.fori_loop(0, 4, functools.partial(turn, stage), 0, unroll=4)

    def tiles(stage, low, high):
        lax.fori_loop(low, high, functools.partial(tile, stage), 0, unroll=4)

    filter_pairs(range(0, 3), *operands)
    pl.semaphore_wait(barrier, 65)
    send_stage(0)
    filter_pairs(range(3, 6), *operands)
    send_stage(1)
    filter_pairs(range(6, 8), *operands)
    send_stage(2)
    first(0, 0, 8)
    second(0)
    first(1, 0, 4)
    arrive(0)
    parameters()
    first(1, 4, 8)
    turns(0)
    tiles(0, 0, 16)
    second(1)
    first(2, 0, 4)
    tiles(0, 16, 32)
    first(2, 4, 8)
    arrive(1)
    turns(1)
    tiles(1, 0, 24)
    second(2)
    tiles(1, 24, 32)
    arrive(2)
    turns(2)

    copies = []
    for k in range(8):
        tiles(2, 4 * k, 4 * k + 4)
        columns, depths = pl.ds((k // 2) * TILE, TILE), pl.ds((k % 2) * 64, 64)
        there = pltpu.make_async_remote_copy(
            part.at[columns, depths], other_ref.at[columns, depths], send.at[k], recv.at[k],
            device_id=(v, mate), device_id_type=MESH,
        )
        here = pltpu.make_async_copy(part.at[columns, depths], own_ref.at[columns, depths], loc.at[k])
        there.start()
        here.start()
        copies += [there, here]
    for copy in copies:
        copy.wait()
    sent = x_ref.at[:, pl.ds(0, 63)]
    pltpu.make_async_copy(sent, sent, a_send).wait()
    half = land.at[:, 0]
    pltpu.make_async_copy(half, half, x_send).wait()
    both = land.at[:, pl.ds(0, 2)]
    pltpu.make_async_copy(both, both, m_send).wait()


def box_kernel(own_ref, other_ref, corner_ref, owner_ref, box_out, vol_out, land, ext, lines, box_ref, vol_ref, sem, out_sem):
    v = lax.axis_index("vol")
    t = lax.axis_index("tilt")
    core = lax.rem(t, 2)
    half = CELLS // 2
    arrive = [
        pltpu.make_async_copy(own_ref, land.at[core], sem.at[core]),
        pltpu.make_async_copy(other_ref, land.at[1 - core], sem.at[1 - core]),
    ]
    for copy in arrive:
        copy.start()
    picks = owner_ref.shape[1]
    owners = [owner_ref[0, r] for r in range(picks)]
    ranks = [sum([(owners[q] == owners[r]).astype(jnp.int32) for q in range(r)], jnp.int32(0)) for r in range(picks)]
    lane = lax.broadcasted_iota(jnp.int32, (BOX, 128), 1)
    y_of = (lane & 63) * 2 + (lane >> 6)
    line = lax.broadcasted_iota(jnp.int32, (BOX, 128), 0)
    quarter = (y_of == line + t * 32).astype(F32).astype(BF)[0:32]
    pltpu.make_async_copy(own_ref, land.at[0], sem.at[0]).wait()

    def slab(i, carry):
        rows = land[0, pl.ds(pl.multiple_of(i * 1024, 1024), 1024), :]
        both = dot_t(quarter, rows)
        for j in range(8):
            lines[pl.ds(i * 8 + j, 32, stride=COLS), :] = both[:, j * 128 : (j + 1) * 128]
        return carry

    lax.fori_loop(0, COLS // 8, slab, 0, unroll=8)
    for i in range(32):
        vol_ref[i] = lines[i * COLS : (i + 1) * COLS, :].astype(BF)
    copies = [pltpu.make_async_copy(vol_ref, vol_out, out_sem.at[4])]
    copies[0].start()
    for side in range(2):
        if side == 1:
            pltpu.make_async_copy(own_ref, land.at[1], sem.at[1]).wait()
        for i in range(8):
            ext[side * half + i * 1024 : side * half + (i + 1) * 1024, :] = land[
                side, i * 1024 : (i + 1) * 1024
            ].astype(F32)

    for slot in range(4):
        mine = [((owners[r] == t) & (ranks[r] == slot)).astype(jnp.int32) for r in range(picks)]
        present = sum(mine)
        x0 = sum([mine[r] * (corner_ref[0, r] - v * COLS) for r in range(picks)])
        y0 = sum([mine[r] * corner_ref[1, r] for r in range(picks)])
        z0 = sum([mine[r] * corner_ref[2, r] for r in range(picks)])
        chosen = ((y_of == line + y0) & (present > 0)).astype(F32).astype(BF)
        origin = x0 * DEPTH + z0

        def cut(i, carry):
            rows = jnp.concatenate(
                [ext[pl.ds(origin + (i * 8 + j) * DEPTH, BOX), :] for j in range(8)], axis=0
            ).astype(BF)
            box_ref[slot, :, pl.ds(pl.multiple_of(i * 512, 512), 512)] = dot_t(chosen, rows).astype(BF)
            return carry

        lax.fori_loop(0, BOX // 8, cut, 0, unroll=8)
        copies.append(pltpu.make_async_copy(box_ref.at[slot], box_out.at[slot], out_sem.at[slot]))
        copies[-1].start()
    for copy in copies:
        copy.wait()


def trig_of(tenths):
    angle = tenths.astype(F32) * (math.pi / 1800.0)
    return jnp.cos(angle), jnp.sin(angle)


def per_device(images, angle_tenths, dose_index, box_corner, box_owner):
    vm = pl.BlockSpec(memory_space=pltpu.VMEM)
    sm = pl.BlockSpec(memory_space=pltpu.SMEM)
    anym = pl.BlockSpec(memory_space=pl.ANY)
    dma = pltpu.SemaphoreType.DMA
    tables = [jnp.asarray(a) for a in fft_tables()]
    lane_tilt = np.zeros(STAGE_LANES[3], np.int32)
    lane_pixel = np.full(STAGE_LANES[3], -1.0e4, np.float32)
    for stage in range(3):
        tilts = [16 * (a % 4) + 4 * g + a // 4 for g in range(4) for a in STAGE_TILTS[stage]]
        at, count = STAGE_LANES[stage], WIN * len(tilts)
        lane_tilt[at : at + count] = np.repeat(np.array(tilts), WIN)
        lane_pixel[at : at + count] = np.tile(np.arange(WIN), len(tilts))
    lane_tilt = jnp.asarray(np.stack([lane_tilt] * 8))
    lane_pixel = jnp.asarray(np.stack([lane_pixel] * 8))
    part, other = pl.pallas_call(
        main_kernel,
        out_shape=(jax.ShapeDtypeStruct((COLS, DEPTH, 128), BF),) * 2,
        in_specs=[vm] * 6 + [sm] * 2 + [vm] * 2,
        out_specs=(anym, anym),
        scratch_shapes=[
            pltpu.VMEM((32 * 32, 128), F32),
            pltpu.VMEM((3 * BLOCKS * STAGE_ROWS, 128), F32),
            pltpu.VMEM((3, BLOCKS, STAGE_ROWS, 128), BF),
            pltpu.VMEM((3, 4, BLOCKS, STAGE_ROWS, 128), BF),
            pltpu.VMEM((4 * BLOCKS * STAGE_ROWS, 128), F32),
            pltpu.VMEM((TILTS * BAND, 128), F32),
            pltpu.VMEM((CELLS // 2, 128), F32),
            pltpu.VMEM((COLS, DEPTH, 128), BF),
            pltpu.VMEM((32, 128), jnp.int32),
            pltpu.SMEM((32, 128), jnp.int32),
            pltpu.VMEM((32, STAGE_LANES[3]), F32),
            pltpu.VMEM((16, STAGE_LANES[3]), F32),
            dma, dma((3, 2, 4)), dma, dma((3, 2, 4)), dma, dma((3,)),
            dma, dma((8,)), dma((8,)), dma((8,)),
        ],
        compiler_params=pltpu.CompilerParams(
            vmem_limit_bytes=VMEM_LIMIT, collective_id=1, has_side_effects=True
        ),
        name="main",
    )(images, *tables, angle_tenths.reshape(1, TILTS_HERE), angle_tenths, dose_index, lane_tilt, lane_pixel)

    boxes, volume = pl.pallas_call(
        box_kernel,
        out_shape=(
            jax.ShapeDtypeStruct((4, BOX, BOX * BOX), BF),
            jax.ShapeDtypeStruct((32, COLS, DEPTH), BF),
        ),
        in_specs=[anym, anym, sm, sm],
        out_specs=(anym, anym),
        scratch_shapes=[
            pltpu.VMEM((2, CELLS // 2, 128), BF),
            pltpu.VMEM((CELLS, 128), F32),
            pltpu.VMEM((32 * COLS, 128), F32),
            pltpu.VMEM((4, BOX, BOX * BOX), BF),
            pltpu.VMEM((32, COLS, DEPTH), BF),
            dma((2,)),
            dma((5,)),
        ],
        compiler_params=pltpu.CompilerParams(vmem_limit_bytes=VMEM_LIMIT),
        name="boxes",
    )(part.reshape(CELLS // 2, 128), other.reshape(CELLS // 2, 128), box_corner, box_owner.T)
    return volume, boxes.reshape(1, 1, 4, BOX, BOX * BOX)


def solution(mesh):
    in_specs = (P("tilt", "vol", None), P("tilt"), P("tilt"), P(None, "vol"), P("vol", None))
    out_specs = (P("tilt", "vol", None), P("vol", "tilt", None, None, None))
    return jax.shard_map(
        per_device, mesh=mesh, in_specs=in_specs, out_specs=out_specs, check_vma=False
    )
```
